32 devices in a mesh: blk: 4 (over y, x), grp: 8 (over z, core).
Axes of the slice: x: 2, y: 2, z: 4, core: 2. Of those that a mesh axis runs over, the one named last changes fastest.
Arguments:
- position: float32 [3, 8192], P(None, ('blk', 'grp'))
- velocity: float32 [3, 8192], P(None, ('blk', 'grp')), may hold values from -3 to 3
- accel_old: float32 [3, 8192], P(None, ('blk', 'grp')), may hold values from -5 to 5
- jerk_old: float32 [3, 8192], P(None, ('blk', 'grp')), may hold values from -5 to 5
- elapsed: float32 [8192], P(('blk', 'grp')), may hold values from 0.01 to 0.1
- masses: float32 [8192], P(('blk', 'grp'))
- active_stars: int32 [1024], P(('blk', 'grp')), may hold values from 0 to 255, as said below
- neighbour_list: int32 [32, 16], P(('blk', 'grp')), may hold values from 0 to 15, as said below
- neighbour_count: int32 [32], P(('blk', 'grp')), may hold values from 1 to 16, as said below
Outputs:
- regular: float32 [6, 1024], P(None, ('blk', 'grp'))
- irregular: float32 [6, 1024], P(None, ('blk', 'grp'))
- correction: float32 [6, 1024], P(None, ('blk', 'grp'))
The draws below stay inside these ranges and needn't reach their ends.
Inputs may be any that keep to these rules, and one draw needn't show every extreme that they name: `active_stars`: the 32 entries of one device are distinct local indices of that device's stars, all inside one block of 128 of them. `neighbour_list`: row r lists neighbour blocks for the active stars of device r, numbered within r's group (2 blocks a device, devices in grp order). Its first neighbour_count[r] entries are distinct and ascending, at most 2 of them from one device, and include the block that holds r's active stars; later entries mean nothing. `neighbour_count`: in every group along blk some device lists 2 blocks of every device of its group.
All inputs are finite; a program needn't handle non-finite values.
Results may differ from the reference program's by a relative error of at most 0.0003.
Values sent between devices are 32-bit elements; how exact they have to be, the bound alone decides.
A program may use at most 64 MiB of HBM per device.

```python
import math
import jax
import jax.numpy as jnp
from jax import lax

RES_DEV = 256
ACT_DEV = 32
BLOCK = 128
NBL = 16
NSTARS = 8192
ACTIVE = 1024
N_BLK = 4
N_GRP = 8


def draw_position(key, part):
    spots = jax.random.uniform(jax.random.fold_in(key, 11), (3, NSTARS), jnp.float32, -1.0, 1.0)
    return spots


def draw_masses(key, part):
    levels = jax.random.uniform(jax.random.fold_in(key, 23), (NSTARS,), jnp.float32, jnp.log(0.3), jnp.log(3.0))
    return jnp.exp(levels) / NSTARS


def list_tables(key):
    owners = N_BLK * N_GRP
    blk_dev = RES_DEV // BLOCK
    keys = jax.random.split(jax.random.fold_in(key, 7001), 8)
    home = jax.random.randint(keys[0], (owners,), 0, blk_dev)
    load = jax.random.randint(keys[1], (owners, 1), 1, 4)
    rolled = jax.random.randint(keys[2], (owners, N_GRP), 0, 4)
    taken = jnp.minimum(2, rolled * load // 3)
    my_slot = jnp.arange(owners) % N_GRP
    holders = jnp.arange(N_GRP)
    is_self = holders[None, :] == my_slot[:, None]
    taken = jnp.where(is_self, jnp.maximum(taken, 1), taken)
    full_owner = jax.random.randint(keys[3], (N_BLK,), 0, N_GRP)
    is_full = my_slot == full_owner[jnp.arange(owners) // N_GRP]
    taken = jnp.where(is_full[:, None], 2, taken)
    first = jax.random.randint(keys[4], (owners, N_GRP), 0, blk_dev)
    first = jnp.where(is_self, home[:, None], first)
    second = (first + 1 + jax.random.randint(keys[5], (owners, N_GRP), 0, blk_dev - 1)) % blk_dev
    slot_low = jnp.where(taken == 2, jnp.minimum(first, second), first)
    slot_high = jnp.maximum(first, second)
    block_ids = jnp.stack([slot_low, slot_high], axis=-1) + holders[None, :, None] * blk_dev
    used = jnp.arange(2)[None, None, :] < taken[:, :, None]
    block_ids = block_ids.reshape(owners, NBL)
    used = used.reshape(owners, NBL)
    place = jnp.cumsum(used.astype(jnp.int32), axis=1) - 1
    target = jnp.where(used, place, NBL)
    filler = jax.random.randint(keys[6], (owners, NBL + 1), 0, N_GRP * blk_dev)
    rows = jnp.arange(owners)[:, None]
    listed = filler.at[rows, target].set(block_ids)[:, :NBL]
    counts = jnp.sum(taken, axis=1).astype(jnp.int32)
    row_keys = jax.random.split(keys[7], owners)
    chosen = jax.vmap(lambda single: jax.random.permutation(single, BLOCK)[:ACT_DEV])(row_keys)
    active = (home[:, None] * BLOCK + chosen).reshape(ACTIVE).astype(jnp.int32)
    return (active, listed.astype(jnp.int32), counts)


def draw_active_stars(key, part):
    return list_tables(key)[0]


def draw_neighbour_list(key, part):
    return list_tables(key)[1]


def draw_neighbour_count(key, part):
    return list_tables(key)[2]


def level_of(key, extent, shards, least, high):
    level, own = 1.0, jax.random.fold_in(key, 6)
    for dim, parts in shards:
        steps = jnp.exp(jax.random.uniform(jax.random.fold_in(own, dim), (parts,), jnp.float32, least / len(shards), high / len(shards)))
        level = level * jnp.repeat(steps, extent[dim] // parts).reshape([-1 if axis == dim else 1 for axis in range(len(extent))])
    return level


def bell_draw(rng, extent, scale, reach, pieces=(), kind=jnp.bfloat16):
    factor_of = level_of(rng, extent, pieces, -0.22, 0.18) if pieces else 1.0
    values = jax.random.normal(rng, extent, jnp.float32) * scale * factor_of
    return jnp.minimum(jnp.maximum(values, -reach), reach).astype(kind)


def setup_inputs(seed: int = 0) -> dict:
    arg_keys = jax.random.split(jax.random.key(seed), 10)
    position = draw_position(jax.random.fold_in(arg_keys[9], 71), 0)
    velocity = bell_draw(arg_keys[1], (3, NSTARS), 0.5, 3.0, ((1, 32),), jnp.float32)
    accel_old = bell_draw(arg_keys[2], (3, NSTARS), 1.0, 5.0, ((1, 32),), jnp.float32)
    jerk_old = bell_draw(arg_keys[3], (3, NSTARS), 1.0, 5.0, ((1, 32),), jnp.float32)
    elapsed = jnp.clip(jnp.exp(math.log(0.1) - 2.3025851 * jax.random.uniform(arg_keys[4], (NSTARS,), jnp.float32) ** level_of(arg_keys[4], (NSTARS,), ((0, 32),), -0.2, 0.2)), 0.01, 0.1)
    masses = draw_masses(jax.random.fold_in(arg_keys[9], 71), 0)
    active_stars = draw_active_stars(jax.random.fold_in(arg_keys[9], 71), 0)
    neighbour_list = draw_neighbour_list(jax.random.fold_in(arg_keys[9], 71), 0)
    neighbour_count = draw_neighbour_count(jax.random.fold_in(arg_keys[9], 71), 0)
    return {"position": position, "velocity": velocity, "accel_old": accel_old, "jerk_old": jerk_old, "elapsed": elapsed, "masses": masses, "active_stars": active_stars, "neighbour_list": neighbour_list, "neighbour_count": neighbour_count}


soften_sq = 0.0001

def two_sums(targets, sources, far_weight, near_weight):
    gap_x = sources[0][None, :] - targets[0][:, None]
    gap_y = sources[1][None, :] - targets[1][:, None]
    gap_z = sources[2][None, :] - targets[2][:, None]
    rel_x = sources[3][None, :] - targets[3][:, None]
    rel_y = sources[4][None, :] - targets[4][:, None]
    rel_z = sources[5][None, :] - targets[5][:, None]
    dist_sq = gap_x * gap_x + gap_y * gap_y + gap_z * gap_z + soften_sq
    inverse = lax.rsqrt(dist_sq)
    inv_cube = inverse * inverse * inverse
    radial = 3.0 * (gap_x * rel_x + gap_y * rel_y + gap_z * rel_z) / dist_sq
    term_list = [gap_x, gap_y, gap_z, rel_x - radial * gap_x, rel_y - radial * gap_y, rel_z - radial * gap_z]
    far_scaled = far_weight * inv_cube
    near_scaled = near_weight * inv_cube
    far_part = jnp.stack([lax.optimization_barrier(jnp.sum(far_scaled * term, axis=1)) for term in term_list])
    near_part = jnp.stack([lax.optimization_barrier(jnp.sum(near_scaled * term, axis=1)) for term in term_list])
    return (far_part, near_part)

def reference(position, velocity, accel_old, jerk_old, elapsed, masses, active_stars, neighbour_list, neighbour_count):
    moved_pos = position + elapsed * (velocity + elapsed * (0.5 * accel_old + elapsed * jerk_old / 6.0))
    turned = velocity + elapsed * (accel_old + 0.5 * elapsed * jerk_old)
    owners = N_BLK * N_GRP
    blk_dev = RES_DEV // BLOCK
    group_blocks = blk_dev * N_GRP
    block_count = NSTARS // BLOCK
    owner_of = jnp.arange(ACTIVE, dtype=jnp.int32) // ACT_DEV
    global_rows = active_stars + owner_of * RES_DEV
    targets = jnp.concatenate([moved_pos[:, global_rows], turned[:, global_rows]], axis=0)
    in_list = jnp.arange(NBL, dtype=jnp.int32)[None, :] < neighbour_count[:, None]
    slot_ids = jnp.where(in_list, neighbour_list, group_blocks)
    owner_rows = jnp.arange(owners, dtype=jnp.int32)[:, None]
    local_member = jnp.zeros((owners, group_blocks + 1), jnp.float32).at[owner_rows, slot_ids].set(1.0)[:, :group_blocks]
    block_ids = jnp.arange(block_count, dtype=jnp.int32)
    same_group = (block_ids // group_blocks)[None, :] == (jnp.arange(owners, dtype=jnp.int32) // N_GRP)[:, None]
    member = jnp.where(same_group, local_member[:, block_ids % group_blocks], 0.0)
    per_batch = 8
    batch_count = owners // per_batch
    piece_size = RES_DEV * 8
    piece_count = NSTARS // piece_size
    target_batches = targets.reshape(6, batch_count, per_batch * ACT_DEV).transpose(1, 0, 2)
    member_batches = member.reshape(batch_count, per_batch, block_count)
    source_all = jnp.concatenate([moved_pos, turned], axis=0).reshape(6, piece_count, piece_size).transpose(1, 0, 2)
    mass_pieces = masses.reshape(piece_count, piece_size)
    piece_index = jnp.arange(piece_count, dtype=jnp.int32)

    def one_batch(items):
        target_block, member_block = items
        row_member = jnp.repeat(member_block, ACT_DEV, axis=0)

        def add_piece(carry, inputs):
            source_block, mass_block, index_now = inputs
            near_blocks = lax.dynamic_slice_in_dim(row_member, index_now * (piece_size // BLOCK), piece_size // BLOCK, 1)
            near_mask = jnp.repeat(near_blocks, BLOCK, axis=1)
            far_part, near_part = two_sums(target_block, source_block, mass_block[None, :] * (1.0 - near_mask), mass_block[None, :] * near_mask)
            return ((carry[0] + far_part, carry[1] + near_part), None)
        zero_sums = jnp.zeros((6, per_batch * ACT_DEV), jnp.float32)
        totals, unused = lax.scan(add_piece, (zero_sums, zero_sums), (source_all, mass_pieces, piece_index))
        return totals
    far_all, near_all = lax.map(one_batch, (target_batches, member_batches))
    regular = far_all.transpose(1, 0, 2).reshape(6, ACTIVE)
    irregular = near_all.transpose(1, 0, 2).reshape(6, ACTIVE)
    accel_now = regular[:3] + irregular[:3]
    jerk_now = regular[3:] + irregular[3:]
    step_time = elapsed[global_rows]
    change = accel_old[:, global_rows] - accel_now
    snap_term = -6.0 * change - step_time * (4.0 * jerk_old[:, global_rows] + 2.0 * jerk_now)
    crackle_term = 12.0 * change + 6.0 * step_time * (jerk_old[:, global_rows] + jerk_now)
    return (regular, irregular, jnp.concatenate([snap_term, crackle_term], axis=0))
```

```python
import functools

import jax
import jax.numpy as jnp
from jax import lax
from jax.experimental import pallas as pl
from jax.experimental.pallas import tpu as pltpu
from jax.sharding import PartitionSpec as P

BLOCK = 128
LANES = 128
SOFTEN_SQ = 0.0001
MESH = pl.DeviceIdType.MESH


def xor(a, b, size):
    out, bit = 0, 1
    while bit < size:
        out = out + ((a // bit + b // bit) % 2) * bit
        bit *= 2
    return out


def pair_terms(target, source):
    gap = [source[c] - target[c] for c in range(3)]
    rel = [source[c + 3] - target[c + 3] for c in range(3)]
    dist_sq = gap[0] * gap[0] + gap[1] * gap[1] + gap[2] * gap[2] + SOFTEN_SQ
    inverse = lax.rsqrt(dist_sq)
    inv_sq = inverse * inverse
    scaled = source[6] * (inv_sq * inverse)
    radial = 3.0 * (gap[0] * rel[0] + gap[1] * rel[1] + gap[2] * rel[2]) * inv_sq
    return [scaled * g for g in gap] + [
        scaled * (r - radial * g) for r, g in zip(rel, gap)
    ]


def kernel(
    n_blk, n_grp,
    pos, vel, acc, jerk, elapsed, masses, active, listing, count,
    regular, irregular, correction,
    src, tgt, spread, far, near, flags, columns, out_tx, out_rx,
    src_send, src_recv, tgt_send, tgt_recv, out_send, out_recv,
):
    blk, grp = lax.axis_index("blk"), lax.axis_index("grp")
    res_dev = pos.shape[1]
    act_dev = active.shape[1]
    blk_dev = res_dev // BLOCK
    per_pack = LANES // act_dev
    packs = n_blk // per_pack

    barrier = pltpu.get_barrier_semaphore()
    for k in range(1, n_grp):
        pl.semaphore_signal(
            barrier, inc=1, device_id=(blk, xor(grp, k, n_grp)), device_id_type=MESH
        )
    for k in range(1, n_blk):
        pl.semaphore_signal(
            barrier, inc=1, device_id=(xor(blk, k, n_blk), grp), device_id_type=MESH
        )

    t = elapsed[...]
    p, v, a, j = pos[...], vel[...], acc[...], jerk[...]
    src[0, 0:3, :] = p + t * (v + t * (0.5 * a + t * j / 6.0))
    src[0, 3:6, :] = v + t * (a + 0.5 * t * j)
    src[0, 6:7, :] = masses[...]
    src[0, 7:8, :] = t

    chosen = jnp.concatenate([active[...]] * per_pack, axis=1)
    chosen = jnp.broadcast_to(chosen, (8, LANES))
    place = chosen % BLOCK
    old = jnp.concatenate([a, j, t, t], axis=0)
    own_new = jnp.zeros((8, LANES), jnp.float32)
    own_old = jnp.zeros((8, LANES), jnp.float32)
    for b in range(blk_dev):
        here = chosen // BLOCK == b
        cut = slice(b * BLOCK, (b + 1) * BLOCK)
        own_new = jnp.where(
            here, jnp.take_along_axis(src[0, :, cut], place, axis=1), own_new
        )
        own_old = jnp.where(
            here, jnp.take_along_axis(old[:, cut], place, axis=1), own_old
        )
    tgt[0] = own_new

    pl.semaphore_wait(barrier, n_grp - 1 + n_blk - 1)

    def tgt_copy(k):
        return pltpu.make_async_remote_copy(
            src_ref=tgt.at[0], dst_ref=tgt.at[k],
            send_sem=tgt_send.at[k], recv_sem=tgt_recv.at[k],
            device_id=(xor(blk, k, n_blk), grp), device_id_type=MESH,
        )

    def src_copy(k):
        return pltpu.make_async_remote_copy(
            src_ref=src.at[0], dst_ref=src.at[k],
            send_sem=src_send.at[k], recv_sem=src_recv.at[k],
            device_id=(blk, xor(grp, k, n_grp)), device_id_type=MESH,
        )

    def out_copy(k):
        pack = k // per_pack
        return pltpu.make_async_remote_copy(
            src_ref=out_tx.at[pack], dst_ref=out_rx.at[k],
            send_sem=out_send.at[k], recv_sem=out_recv.at[k],
            device_id=(xor(blk, k, n_blk), grp), device_id_type=MESH,
        )

    for k in range(1, n_blk):
        tgt_copy(k).start()
    for k in reversed(range(1, n_grp)):
        src_copy(k).start()

    slots = listing.shape[1]
    names = lax.broadcasted_iota(jnp.int32, (blk_dev * n_grp, slots), 0)
    spots = lax.broadcasted_iota(jnp.int32, (blk_dev * n_grp, slots), 1)
    hit = (listing[...] == names) & (spots < count[...])
    member = jnp.max(jnp.where(hit, 1.0, 0.0), axis=1, keepdims=True)
    flags[...] = jnp.broadcast_to(member, flags.shape)

    for k in range(1, n_blk):
        tgt_copy(k).wait_recv()
    lane = lax.broadcasted_iota(jnp.int32, (8, LANES), 1)
    for pack in range(packs):
        mixed = tgt[pack * per_pack]
        for i in range(1, per_pack):
            mixed = jnp.where(lane >= i * act_dev, tgt[pack * per_pack + i], mixed)
        turned = mixed.T
        for c in range(6):
            spread[c, pack * LANES : (pack + 1) * LANES, :] = jnp.broadcast_to(
                turned[:, c : c + 1], (LANES, LANES)
            )

    def add_block(k, first):
        source = [
            [src[k, c : c + 1, b * BLOCK : (b + 1) * BLOCK] for c in range(7)]
            for b in range(blk_dev)
        ]

        def far_slot(slot, carry):
            rows = pl.ds(pl.multiple_of(slot * act_dev, act_dev), act_dev)
            target = [spread[c, rows, :] for c in range(6)]
            terms = pair_terms(target, source[0])
            for b in range(1, blk_dev):
                terms = [x + y for x, y in zip(terms, pair_terms(target, source[b]))]
            for c in range(6):
                far[c, rows, :] = terms[c] if first else far[c, rows, :] + terms[c]
            return carry

        rows = slice(0, act_dev)
        target = [spread[c, rows, :] for c in range(6)]
        far_sum = [0.0 if first else far[c, rows, :] for c in range(6)]
        near_sum = [0.0 if first else near[c] for c in range(6)]
        for b in range(blk_dev):
            block_id = xor(grp, k, n_grp) * blk_dev + b
            is_near = flags[pl.ds(block_id, 1), :]
            for c, term in enumerate(pair_terms(target, source[b])):
                kept = term * is_near
                near_sum[c] = near_sum[c] + kept
                far_sum[c] = far_sum[c] + (term - kept)
        for c in range(6):
            far[c, rows, :] = far_sum[c]
            near[c] = near_sum[c]
        lax.fori_loop(1, n_blk, far_slot, 0)

    add_block(0, True)

    def later(k, carry):
        src_copy(k).wait_recv()
        add_block(k, False)
        return carry

    lax.fori_loop(1, n_grp, later, 0)

    for pack in range(packs):
        rows = slice(pack * LANES, (pack + 1) * LANES)
        lanes = lax.broadcasted_iota(jnp.int32, (LANES, LANES), 1)
        packed = jnp.zeros((LANES, LANES), jnp.float32)
        for c in range(6):
            total = jnp.sum(far[c, rows, :], axis=1, keepdims=True)
            packed = jnp.where(lanes == c, total, packed)
        columns[...] = packed
        if pack == 0:
            mine = columns[0:act_dev, :]
            for c in range(6):
                total = jnp.sum(near[c], axis=1, keepdims=True)
                mine = jnp.where(lanes[:act_dev] == c + 8, total, mine)
            columns[0:act_dev, :] = mine
        flat = columns[...].T
        out_tx[pack] = flat[0:8, :]
        if pack == 0:
            irr = flat[8:14, 0:act_dev]
        for k in range(max(1, pack * per_pack), (pack + 1) * per_pack):
            out_copy(k).start()

    reg = out_tx[0][0:6, 0:act_dev]
    irregular[...] = irr
    for k in range(1, n_blk):
        out_copy(k).wait_recv()
        left = (k % per_pack) * act_dev
        reg = reg + out_rx[k][0:6, left : left + act_dev]
    regular[...] = reg
    total = reg + irr
    accel_now, jerk_now = total[0:3], total[3:6]
    mine = own_old[:, 0:act_dev]
    start_accel, start_jerk, step = mine[0:3], mine[3:6], mine[6:7]
    change = start_accel - accel_now
    correction[0:3, :] = -6.0 * change - step * (4.0 * start_jerk + 2.0 * jerk_now)
    correction[3:6, :] = 12.0 * change + 6.0 * step * (start_jerk + jerk_now)

    for k in range(1, n_blk):
        tgt_copy(k).wait_send()
        out_copy(k).wait_send()
    for k in range(1, n_grp):
        src_copy(k).wait_send()


def per_device(
    n_blk, n_grp,
    position, velocity, accel_old, jerk_old, elapsed, masses,
    active_stars, neighbour_list, neighbour_count,
):
    act_dev = active_stars.shape[0]
    res_dev = position.shape[1]
    packs = n_blk * act_dev // LANES
    shape = jax.ShapeDtypeStruct((6, act_dev), jnp.float32)
    vmem = pl.BlockSpec(memory_space=pltpu.VMEM)
    f32 = jnp.float32
    return pl.pallas_call(
        functools.partial(kernel, n_blk, n_grp),
        out_shape=(shape, shape, shape),
        in_specs=[vmem] * 9,
        out_specs=(vmem, vmem, vmem),
        scratch_shapes=[
            pltpu.VMEM((n_grp, 8, res_dev), f32),
            pltpu.VMEM((n_blk, 8, LANES), f32),
            pltpu.VMEM((6, packs * LANES, LANES), f32),
            pltpu.VMEM((6, packs * LANES, LANES), f32),
            pltpu.VMEM((6, act_dev, LANES), f32),
            pltpu.VMEM((n_grp * res_dev // BLOCK, LANES), f32),
            pltpu.VMEM((LANES, LANES), f32),
            pltpu.VMEM((packs, 8, LANES), f32),
            pltpu.VMEM((n_blk, 8, LANES), f32),
            pltpu.SemaphoreType.DMA((n_grp,)),
            pltpu.SemaphoreType.DMA((n_grp,)),
            pltpu.SemaphoreType.DMA((n_blk,)),
            pltpu.SemaphoreType.DMA((n_blk,)),
            pltpu.SemaphoreType.DMA((n_blk,)),
            pltpu.SemaphoreType.DMA((n_blk,)),
        ],
        compiler_params=pltpu.CompilerParams(collective_id=0, has_side_effects=True),
        cost_estimate=pl.CostEstimate(
            flops=40 * n_blk * act_dev * n_grp * res_dev,
            bytes_accessed=32 * res_dev * n_grp,
            transcendentals=n_blk * act_dev * n_grp * res_dev,
        ),
    )(
        position, velocity, accel_old, jerk_old,
        elapsed.reshape(1, -1), masses.reshape(1, -1), active_stars.reshape(1, -1),
        neighbour_list, neighbour_count.reshape(1, -1),
    )


def solution(mesh):
    stars = P(None, ("blk", "grp"))
    flat = P(("blk", "grp"))
    return jax.shard_map(
        functools.partial(per_device, mesh.shape["blk"], mesh.shape["grp"]),
        mesh=mesh,
        in_specs=(stars,) * 4 + (flat,) * 3 + (P(("blk", "grp"), None), flat),
        out_specs=(stars,) * 3,
        check_vma=False,
    )
```

```python
import functools

import jax
import jax.numpy as jnp
from jax import lax
from jax.experimental import pallas as pl
from jax.experimental.pallas import tpu as pltpu
from jax.sharding import PartitionSpec as P

BLOCK = 128
LANES = 128
SOFTEN_SQ = 0.0001
MESH = pl.DeviceIdType.MESH


def xor(a, b, size):
    out, bit = 0, 1
    while bit < size:
        out = out + ((a // bit + b // bit) % 2) * bit
        bit *= 2
    return out


def pair_terms(target, source):
    gap = [source[c] - target[c] for c in range(3)]
    rel = [source[c + 3] - target[c + 3] for c in range(3)]
    dist_sq = gap[0] * gap[0] + gap[1] * gap[1] + gap[2] * gap[2] + SOFTEN_SQ
    inverse = lax.rsqrt(dist_sq)
    inv_sq = inverse * inverse
    scaled = source[6] * (inv_sq * inverse)
    radial = 3.0 * (gap[0] * rel[0] + gap[1] * rel[1] + gap[2] * rel[2]) * inv_sq
    return [scaled * g for g in gap] + [
        scaled * (r - radial * g) for r, g in zip(rel, gap)
    ]


def kernel(
    n_blk, n_grp,
    pos_hbm, vel_hbm, acc_hbm, jerk_hbm, elapsed_hbm, masses_hbm, active_hbm,
    listing_hbm, count_hbm, result,
    pos, vel, acc, jerk, elapsed, masses, active, listing, count, in_sem,
    src, tgt, spread, far, near, flags, columns, out_tx, out_rx,
    src_send, src_recv, tgt_send, tgt_recv, out_send, out_recv,
):
    blk, grp = lax.axis_index("blk"), lax.axis_index("grp")
    res_dev = pos.shape[1]
    act_dev = active.shape[1]
    blk_dev = res_dev // BLOCK
    per_pack = LANES // act_dev
    packs = n_blk // per_pack

    barrier = pltpu.get_barrier_semaphore()
    for k in range(1, n_grp):
        pl.semaphore_signal(
            barrier, inc=1, device_id=(blk, xor(grp, k, n_grp)), device_id_type=MESH
        )
    for k in range(1, n_blk):
        pl.semaphore_signal(
            barrier, inc=1, device_id=(xor(blk, k, n_blk), grp), device_id_type=MESH
        )

    loads = [
        pltpu.make_async_copy(there, here, in_sem.at[i])
        for i, (there, here) in enumerate(
            (
                (pos_hbm, pos), (vel_hbm, vel), (acc_hbm, acc), (jerk_hbm, jerk),
                (elapsed_hbm, elapsed), (masses_hbm, masses), (active_hbm, active),
                (listing_hbm, listing), (count_hbm, count),
            )
        )
    ]
    for load in loads:
        load.start()
    for load in loads:
        load.wait()
    t = elapsed[...]
    p, v, a, j = pos[...], vel[...], acc[...], jerk[...]
    src[0, 0:3, :] = p + t * (v + t * (0.5 * a + t * j / 6.0))
    src[0, 3:6, :] = v + t * (a + 0.5 * t * j)
    src[0, 6:7, :] = masses[...]
    src[0, 7:8, :] = t

    chosen = jnp.concatenate([active[...]] * per_pack, axis=1)
    chosen = jnp.broadcast_to(chosen, (8, LANES))
    place = chosen % BLOCK
    old = jnp.concatenate([a, j, t, t], axis=0)
    own_new = jnp.zeros((8, LANES), jnp.float32)
    own_old = jnp.zeros((8, LANES), jnp.float32)
    for b in range(blk_dev):
        here = chosen // BLOCK == b
        cut = slice(b * BLOCK, (b + 1) * BLOCK)
        own_new = jnp.where(
            here, jnp.take_along_axis(src[0, :, cut], place, axis=1), own_new
        )
        own_old = jnp.where(
            here, jnp.take_along_axis(old[:, cut], place, axis=1), own_old
        )
    tgt[0] = own_new

    pl.semaphore_wait(barrier, n_grp - 1 + n_blk - 1)

    def tgt_copy(k):
        return pltpu.make_async_remote_copy(
            src_ref=tgt.at[0], dst_ref=tgt.at[k],
            send_sem=tgt_send.at[k], recv_sem=tgt_recv.at[k],
            device_id=(xor(blk, k, n_blk), grp), device_id_type=MESH,
        )

    def src_copy(k):
        return pltpu.make_async_remote_copy(
            src_ref=src.at[0], dst_ref=src.at[k],
            send_sem=src_send.at[k], recv_sem=src_recv.at[k],
            device_id=(blk, xor(grp, k, n_grp)), device_id_type=MESH,
        )

    def out_copy(k):
        pack = k // per_pack
        return pltpu.make_async_remote_copy(
            src_ref=out_tx.at[pack], dst_ref=out_rx.at[k],
            send_sem=out_send.at[k], recv_sem=out_recv.at[k],
            device_id=(xor(blk, k, n_blk), grp), device_id_type=MESH,
        )

    for k in range(1, n_blk):
        tgt_copy(k).start()
    for k in reversed(range(1, n_grp)):
        src_copy(k).start()

    slots = listing.shape[1]
    names = lax.broadcasted_iota(jnp.int32, (blk_dev * n_grp, slots), 0)
    spots = lax.broadcasted_iota(jnp.int32, (blk_dev * n_grp, slots), 1)
    hit = (listing[...] == names) & (spots < count[0])
    member = jnp.max(jnp.where(hit, 1.0, 0.0), axis=1, keepdims=True)
    flags[...] = jnp.broadcast_to(member, flags.shape)

    for k in range(1, n_blk):
        tgt_copy(k).wait_recv()
    lane = lax.broadcasted_iota(jnp.int32, (8, LANES), 1)
    for pack in range(packs):
        mixed = tgt[pack * per_pack]
        for i in range(1, per_pack):
            mixed = jnp.where(lane >= i * act_dev, tgt[pack * per_pack + i], mixed)
        turned = mixed.T
        for c in range(6):
            spread[c, pack * LANES : (pack + 1) * LANES, :] = jnp.broadcast_to(
                turned[:, c : c + 1], (LANES, LANES)
            )

    def add_block(k, first):
        source = [
            [src[k, c : c + 1, b * BLOCK : (b + 1) * BLOCK] for c in range(7)]
            for b in range(blk_dev)
        ]

        def far_slot(slot, carry):
            rows = pl.ds(pl.multiple_of(slot * act_dev, act_dev), act_dev)
            target = [spread[c, rows, :] for c in range(6)]
            terms = pair_terms(target, source[0])
            for b in range(1, blk_dev):
                terms = [x + y for x, y in zip(terms, pair_terms(target, source[b]))]
            for c in range(6):
                far[c, rows, :] = terms[c] if first else far[c, rows, :] + terms[c]
            return carry

        rows = slice(0, act_dev)
        target = [spread[c, rows, :] for c in range(6)]
        far_sum = [0.0 if first else far[c, rows, :] for c in range(6)]
        near_sum = [0.0 if first else near[c] for c in range(6)]
        for b in range(blk_dev):
            block_id = xor(grp, k, n_grp) * blk_dev + b
            is_near = flags[pl.ds(block_id, 1), :]
            for c, term in enumerate(pair_terms(target, source[b])):
                kept = term * is_near
                near_sum[c] = near_sum[c] + kept
                far_sum[c] = far_sum[c] + (term - kept)
        for c in range(6):
            far[c, rows, :] = far_sum[c]
            near[c] = near_sum[c]
        lax.fori_loop(1, n_blk, far_slot, 0)

    add_block(0, True)

    def later(k, carry):
        src_copy(k).wait_recv()
        add_block(k, False)
        return carry

    lax.fori_loop(1, n_grp, later, 0)

    for pack in range(packs):
        rows = slice(pack * LANES, (pack + 1) * LANES)
        lanes = lax.broadcasted_iota(jnp.int32, (LANES, LANES), 1)
        packed = jnp.zeros((LANES, LANES), jnp.float32)
        for c in range(6):
            total = jnp.sum(far[c, rows, :], axis=1, keepdims=True)
            packed = jnp.where(lanes == c, total, packed)
        columns[...] = packed
        if pack == 0:
            mine = columns[0:act_dev, :]
            for c in range(6):
                total = jnp.sum(near[c], axis=1, keepdims=True)
                mine = jnp.where(lanes[:act_dev] == c + 8, total, mine)
            columns[0:act_dev, :] = mine
        flat = columns[...].T
        out_tx[pack] = flat[0:8, :]
        if pack == 0:
            irr = flat[8:14, 0:act_dev]
        for k in range(max(1, pack * per_pack), (pack + 1) * per_pack):
            out_copy(k).start()

    reg = out_tx[0][0:6, 0:act_dev]
    result[8:14, 0:act_dev] = irr
    for k in range(1, n_blk):
        out_copy(k).wait_recv()
        left = (k % per_pack) * act_dev
        reg = reg + out_rx[k][0:6, left : left + act_dev]
    result[0:6, 0:act_dev] = reg
    total = reg + irr
    accel_now, jerk_now = total[0:3], total[3:6]
    mine = own_old[:, 0:act_dev]
    start_accel, start_jerk, step = mine[0:3], mine[3:6], mine[6:7]
    change = start_accel - accel_now
    result[16:19, 0:act_dev] = -6.0 * change - step * (4.0 * start_jerk + 2.0 * jerk_now)
    result[19:22, 0:act_dev] = 12.0 * change + 6.0 * step * (start_jerk + jerk_now)

    for k in range(1, n_blk):
        tgt_copy(k).wait_send()
        out_copy(k).wait_send()
    for k in range(1, n_grp):
        src_copy(k).wait_send()


def write_out(result, regular, irregular, correction):
    act_dev = regular.shape[1]
    regular[...] = result[0:6, 0:act_dev]
    irregular[...] = result[8:14, 0:act_dev]
    correction[...] = result[16:22, 0:act_dev]


def per_device(
    n_blk, n_grp,
    position, velocity, accel_old, jerk_old, elapsed, masses,
    active_stars, neighbour_list, neighbour_count,
):
    act_dev = active_stars.shape[0]
    res_dev = position.shape[1]
    packs = n_blk * act_dev // LANES
    shape = jax.ShapeDtypeStruct((6, act_dev), jnp.float32)
    vmem = pl.BlockSpec(memory_space=pltpu.VMEM)
    f32 = jnp.float32
    result = pl.pallas_call(
        functools.partial(kernel, n_blk, n_grp),
        out_shape=pltpu.VMEM((24, LANES), f32),
        in_specs=[pl.BlockSpec(memory_space=pltpu.HBM)] * 9,
        out_specs=vmem,
        scratch_shapes=[
            pltpu.VMEM(position.shape, f32),
            pltpu.VMEM(position.shape, f32),
            pltpu.VMEM(position.shape, f32),
            pltpu.VMEM(position.shape, f32),
            pltpu.VMEM((1, res_dev), f32),
            pltpu.VMEM((1, res_dev), f32),
            pltpu.VMEM((1, act_dev), jnp.int32),
            pltpu.VMEM(neighbour_list.shape, jnp.int32),
            pltpu.SMEM((1,), jnp.int32),
            pltpu.SemaphoreType.DMA((9,)),
            pltpu.VMEM((n_grp, 8, res_dev), f32),
            pltpu.VMEM((n_blk, 8, LANES), f32),
            pltpu.VMEM((6, packs * LANES, LANES), f32),
            pltpu.VMEM((6, packs * LANES, LANES), f32),
            pltpu.VMEM((6, act_dev, LANES), f32),
            pltpu.VMEM((n_grp * res_dev // BLOCK, LANES), f32),
            pltpu.VMEM((LANES, LANES), f32),
            pltpu.VMEM((packs, 8, LANES), f32),
            pltpu.VMEM((n_blk, 8, LANES), f32),
            pltpu.SemaphoreType.DMA((n_grp,)),
            pltpu.SemaphoreType.DMA((n_grp,)),
            pltpu.SemaphoreType.DMA((n_blk,)),
            pltpu.SemaphoreType.DMA((n_blk,)),
            pltpu.SemaphoreType.DMA((n_blk,)),
            pltpu.SemaphoreType.DMA((n_blk,)),
        ],
        compiler_params=pltpu.CompilerParams(collective_id=0, has_side_effects=True),
        cost_estimate=pl.CostEstimate(
            flops=40 * n_blk * act_dev * n_grp * res_dev,
            bytes_accessed=32 * res_dev * n_grp,
            transcendentals=n_blk * act_dev * n_grp * res_dev,
        ),
    )(
        position, velocity, accel_old, jerk_old,
        elapsed.reshape(1, -1), masses.reshape(1, -1), active_stars.reshape(1, -1),
        neighbour_list, neighbour_count,
    )
    return pl.pallas_call(
        write_out,
        out_shape=(shape, shape, shape),
        in_specs=[vmem],
        out_specs=(vmem, vmem, vmem),
    )(result)


def solution(mesh):
    stars = P(None, ("blk", "grp"))
    flat = P(("blk", "grp"))
    return jax.shard_map(
        functools.partial(per_device, mesh.shape["blk"], mesh.shape["grp"]),
        mesh=mesh,
        in_specs=(stars,) * 4 + (flat,) * 3 + (P(("blk", "grp"), None), flat),
        out_specs=(stars,) * 3,
        check_vma=False,
    )
```

```python
import functools

import jax
import jax.numpy as jnp
from jax import lax
from jax.experimental import pallas as pl
from jax.experimental.pallas import tpu as pltpu
from jax.sharding import PartitionSpec as P

BLOCK = 128
LANES = 128
SOFTEN_SQ = 0.0001
MESH = pl.DeviceIdType.MESH


def xor(a, b, size):
    out, bit = 0, 1
    while bit < size:
        out = out + ((a // bit + b // bit) % 2) * bit
        bit *= 2
    return out


def pair_terms(target, source):
    gap = [source[c] - target[c] for c in range(3)]
    rel = [source[c + 3] - target[c + 3] for c in range(3)]
    dist_sq = gap[0] * gap[0] + gap[1] * gap[1] + gap[2] * gap[2] + SOFTEN_SQ
    inverse = lax.rsqrt(dist_sq)
    inv_sq = inverse * inverse
    scaled = source[6] * (inv_sq * inverse)
    radial = (gap[0] * rel[0] + gap[1] * rel[1] + gap[2] * rel[2]) * (3.0 * inv_sq)
    return [scaled * g for g in gap] + [
        scaled * (r - radial * g) for r, g in zip(rel, gap)
    ]


def kernel(
    n_blk, n_grp,
    pos_hbm, vel_hbm, acc_hbm, jerk_hbm, elapsed_hbm, masses_hbm, active_hbm,
    listing_hbm, count_hbm, result,
    pos, vel, acc, jerk, elapsed, masses, active, listing, count, in_sem,
    src, tgt, spread, far, near, flags, columns, out_tx, out_rx,
    src_send, src_recv, tgt_send, tgt_recv, out_send, out_recv,
):
    blk, grp = lax.axis_index("blk"), lax.axis_index("grp")
    res_dev = pos.shape[1]
    act_dev = active.shape[1]
    blk_dev = res_dev // BLOCK
    per_pack = LANES // act_dev
    packs = n_blk // per_pack

    barrier = pltpu.get_barrier_semaphore()
    for k in range(1, n_grp):
        pl.semaphore_signal(
            barrier, inc=1, device_id=(blk, xor(grp, k, n_grp)), device_id_type=MESH
        )
    for k in range(1, n_blk):
        pl.semaphore_signal(
            barrier, inc=1, device_id=(xor(blk, k, n_blk), grp), device_id_type=MESH
        )

    loads = [
        pltpu.make_async_copy(there, here, in_sem.at[i])
        for i, (there, here) in enumerate(
            (
                (pos_hbm, pos), (vel_hbm, vel), (acc_hbm, acc), (jerk_hbm, jerk),
                (elapsed_hbm, elapsed), (masses_hbm, masses), (active_hbm, active),
                (listing_hbm, listing), (count_hbm, count),
            )
        )
    ]
    for load in loads:
        load.start()
    for load in loads:
        load.wait()
    t = elapsed[...]
    p, v, a, j = pos[...], vel[...], acc[...], jerk[...]
    src[0, 0:3, :] = p + t * (v + t * (0.5 * a + t * j / 6.0))
    src[0, 3:6, :] = v + t * (a + 0.5 * t * j)
    src[0, 6:7, :] = masses[...]
    src[0, 7:8, :] = t

    chosen = jnp.concatenate([active[...]] * per_pack, axis=1)
    chosen = jnp.broadcast_to(chosen, (8, LANES))
    place = chosen % BLOCK
    old = jnp.concatenate([a, j, t, t], axis=0)
    own_new = jnp.zeros((8, LANES), jnp.float32)
    own_old = jnp.zeros((8, LANES), jnp.float32)
    for b in range(blk_dev):
        here = chosen // BLOCK == b
        cut = slice(b * BLOCK, (b + 1) * BLOCK)
        own_new = jnp.where(
            here, jnp.take_along_axis(src[0, :, cut], place, axis=1), own_new
        )
        own_old = jnp.where(
            here, jnp.take_along_axis(old[:, cut], place, axis=1), own_old
        )
    tgt[0] = own_new

    pl.semaphore_wait(barrier, n_grp - 1 + n_blk - 1)

    def tgt_copy(k):
        return pltpu.make_async_remote_copy(
            src_ref=tgt.at[0], dst_ref=tgt.at[k],
            send_sem=tgt_send.at[k], recv_sem=tgt_recv.at[k],
            device_id=(xor(blk, k, n_blk), grp), device_id_type=MESH,
        )

    def src_copy(k):
        return pltpu.make_async_remote_copy(
            src_ref=src.at[0], dst_ref=src.at[k],
            send_sem=src_send.at[k], recv_sem=src_recv.at[k],
            device_id=(blk, xor(grp, k, n_grp)), device_id_type=MESH,
        )

    def out_copy(k):
        pack = k // per_pack
        return pltpu.make_async_remote_copy(
            src_ref=out_tx.at[pack], dst_ref=out_rx.at[k],
            send_sem=out_send.at[k], recv_sem=out_recv.at[k],
            device_id=(xor(blk, k, n_blk), grp), device_id_type=MESH,
        )

    for k in range(1, n_blk):
        tgt_copy(k).start()
    for k in reversed(range(1, n_grp)):
        src_copy(k).start()

    slots = listing.shape[1]
    names = lax.broadcasted_iota(jnp.int32, (blk_dev * n_grp, slots), 0)
    spots = lax.broadcasted_iota(jnp.int32, (blk_dev * n_grp, slots), 1)
    hit = (listing[...] == names) & (spots < count[0])
    member = jnp.max(jnp.where(hit, 1.0, 0.0), axis=1, keepdims=True)
    flags[...] = jnp.broadcast_to(member, flags.shape)

    for k in range(1, n_blk):
        tgt_copy(k).wait_recv()
    lane = lax.broadcasted_iota(jnp.int32, (8, LANES), 1)
    for pack in range(packs):
        mixed = tgt[pack * per_pack]
        for i in range(1, per_pack):
            mixed = jnp.where(lane >= i * act_dev, tgt[pack * per_pack + i], mixed)
        turned = mixed.T
        for c in range(6):
            spread[c, pack * LANES : (pack + 1) * LANES, :] = jnp.broadcast_to(
                turned[:, c : c + 1], (LANES, LANES)
            )

    def add_block(k, first):
        source = [
            [src[k, c : c + 1, b * BLOCK : (b + 1) * BLOCK] for c in range(7)]
            for b in range(blk_dev)
        ]

        def far_slot(slot, carry):
            rows = pl.ds(pl.multiple_of(slot * act_dev, act_dev), act_dev)
            target = [spread[c, rows, :] for c in range(6)]
            terms = pair_terms(target, source[0])
            for b in range(1, blk_dev):
                terms = [x + y for x, y in zip(terms, pair_terms(target, source[b]))]
            for c in range(6):
                far[c, rows, :] = terms[c] if first else far[c, rows, :] + terms[c]
            return carry

        rows = slice(0, act_dev)
        target = [spread[c, rows, :] for c in range(6)]
        far_sum = [0.0 if first else far[c, rows, :] for c in range(6)]
        near_sum = [0.0 if first else near[c] for c in range(6)]
        for b in range(blk_dev):
            block_id = xor(grp, k, n_grp) * blk_dev + b
            is_near = flags[pl.ds(block_id, 1), :]
            for c, term in enumerate(pair_terms(target, source[b])):
                kept = term * is_near
                near_sum[c] = near_sum[c] + kept
                far_sum[c] = far_sum[c] + (term - kept)
        for c in range(6):
            far[c, rows, :] = far_sum[c]
            near[c] = near_sum[c]
        lax.fori_loop(1, n_blk, far_slot, 0, unroll=True)

    add_block(0, True)

    def later(k, carry):
        src_copy(k).wait_recv()
        add_block(k, False)
        return carry

    lax.fori_loop(1, n_grp, later, 0)

    for pack in range(packs):
        rows = slice(pack * LANES, (pack + 1) * LANES)
        lanes = lax.broadcasted_iota(jnp.int32, (LANES, LANES), 1)
        packed = jnp.zeros((LANES, LANES), jnp.float32)
        for c in range(6):
            total = jnp.sum(far[c, rows, :], axis=1, keepdims=True)
            packed = jnp.where(lanes == c, total, packed)
        columns[...] = packed
        if pack == 0:
            mine = columns[0:act_dev, :]
            for c in range(6):
                total = jnp.sum(near[c], axis=1, keepdims=True)
                mine = jnp.where(lanes[:act_dev] == c + 8, total, mine)
            columns[0:act_dev, :] = mine
        flat = columns[...].T
        out_tx[pack] = flat[0:8, :]
        if pack == 0:
            irr = flat[8:14, 0:act_dev]
        for k in range(max(1, pack * per_pack), (pack + 1) * per_pack):
            out_copy(k).start()

    reg = out_tx[0][0:6, 0:act_dev]
    result[8:14, 0:act_dev] = irr
    for k in range(1, n_blk):
        out_copy(k).wait_recv()
        left = (k % per_pack) * act_dev
        reg = reg + out_rx[k][0:6, left : left + act_dev]
    result[0:6, 0:act_dev] = reg
    total = reg + irr
    accel_now, jerk_now = total[0:3], total[3:6]
    mine = own_old[:, 0:act_dev]
    start_accel, start_jerk, step = mine[0:3], mine[3:6], mine[6:7]
    change = start_accel - accel_now
    result[16:19, 0:act_dev] = -6.0 * change - step * (4.0 * start_jerk + 2.0 * jerk_now)
    result[19:22, 0:act_dev] = 12.0 * change + 6.0 * step * (start_jerk + jerk_now)

    for k in range(1, n_blk):
        tgt_copy(k).wait_send()
        out_copy(k).wait_send()
    for k in range(1, n_grp):
        src_copy(k).wait_send()


def write_out(result, regular, irregular, correction):
    act_dev = regular.shape[1]
    regular[...] = result[0:6, 0:act_dev]
    irregular[...] = result[8:14, 0:act_dev]
    correction[...] = result[16:22, 0:act_dev]


def per_device(
    n_blk, n_grp,
    position, velocity, accel_old, jerk_old, elapsed, masses,
    active_stars, neighbour_list, neighbour_count,
):
    act_dev = active_stars.shape[0]
    res_dev = position.shape[1]
    packs = n_blk * act_dev // LANES
    shape = jax.ShapeDtypeStruct((6, act_dev), jnp.float32)
    vmem = pl.BlockSpec(memory_space=pltpu.VMEM)
    f32 = jnp.float32
    result = pl.pallas_call(
        functools.partial(kernel, n_blk, n_grp),
        out_shape=pltpu.VMEM((24, LANES), f32),
        in_specs=[pl.BlockSpec(memory_space=pltpu.HBM)] * 9,
        out_specs=vmem,
        scratch_shapes=[
            pltpu.VMEM(position.shape, f32),
            pltpu.VMEM(position.shape, f32),
            pltpu.VMEM(position.shape, f32),
            pltpu.VMEM(position.shape, f32),
            pltpu.VMEM((1, res_dev), f32),
            pltpu.VMEM((1, res_dev), f32),
            pltpu.VMEM((1, act_dev), jnp.int32),
            pltpu.VMEM(neighbour_list.shape, jnp.int32),
            pltpu.SMEM((1,), jnp.int32),
            pltpu.SemaphoreType.DMA((9,)),
            pltpu.VMEM((n_grp, 8, res_dev), f32),
            pltpu.VMEM((n_blk, 8, LANES), f32),
            pltpu.VMEM((6, packs * LANES, LANES), f32),
            pltpu.VMEM((6, packs * LANES, LANES), f32),
            pltpu.VMEM((6, act_dev, LANES), f32),
            pltpu.VMEM((n_grp * res_dev // BLOCK, LANES), f32),
            pltpu.VMEM((LANES, LANES), f32),
            pltpu.VMEM((packs, 8, LANES), f32),
            pltpu.VMEM((n_blk, 8, LANES), f32),
            pltpu.SemaphoreType.DMA((n_grp,)),
            pltpu.SemaphoreType.DMA((n_grp,)),
            pltpu.SemaphoreType.DMA((n_blk,)),
            pltpu.SemaphoreType.DMA((n_blk,)),
            pltpu.SemaphoreType.DMA((n_blk,)),
            pltpu.SemaphoreType.DMA((n_blk,)),
        ],
        compiler_params=pltpu.CompilerParams(collective_id=0, has_side_effects=True),
        cost_estimate=pl.CostEstimate(
            flops=40 * n_blk * act_dev * n_grp * res_dev,
            bytes_accessed=32 * res_dev * n_grp,
            transcendentals=n_blk * act_dev * n_grp * res_dev,
        ),
    )(
        position, velocity, accel_old, jerk_old,
        elapsed.reshape(1, -1), masses.reshape(1, -1), active_stars.reshape(1, -1),
        neighbour_list, neighbour_count,
    )
    return pl.pallas_call(
        write_out,
        out_shape=(shape, shape, shape),
        in_specs=[vmem],
        out_specs=(vmem, vmem, vmem),
    )(pltpu.with_memory_space_constraint(result, pltpu.VMEM))


def solution(mesh):
    stars = P(None, ("blk", "grp"))
    flat = P(("blk", "grp"))
    return jax.shard_map(
        functools.partial(per_device, mesh.shape["blk"], mesh.shape["grp"]),
        mesh=mesh,
        in_specs=(stars,) * 4 + (flat,) * 3 + (P(("blk", "grp"), None), flat),
        out_specs=(stars,) * 3,
        check_vma=False,
    )
```

```python
import functools

import jax
import jax.numpy as jnp
from jax import lax
from jax.experimental import pallas as pl
from jax.experimental.pallas import tpu as pltpu
from jax.sharding import PartitionSpec as P

BLOCK = 128
LANES = 128
SOFTEN_SQ = 0.0001
MESH = pl.DeviceIdType.MESH


def xor(a, b, size):
    out, bit = 0, 1
    while bit < size:
        out = out + ((a // bit + b // bit) % 2) * bit
        bit *= 2
    return out


def pair_terms(target, source):
    gap = [source[c] - target[c] for c in range(3)]
    rel = [source[c + 3] - target[c + 3] for c in range(3)]
    dist_sq = gap[0] * gap[0] + gap[1] * gap[1] + gap[2] * gap[2] + SOFTEN_SQ
    inverse = lax.rsqrt(dist_sq)
    inv_sq = inverse * inverse
    scaled = source[6] * (inv_sq * inverse)
    radial = (gap[0] * rel[0] + gap[1] * rel[1] + gap[2] * rel[2]) * (3.0 * inv_sq)
    return [scaled * g for g in gap] + [
        scaled * (r - radial * g) for r, g in zip(rel, gap)
    ]


def kernel(
    n_blk, n_grp,
    pos_hbm, vel_hbm, acc_hbm, jerk_hbm, elapsed_hbm, masses_hbm, active_hbm,
    listing_hbm, count_hbm, result,
    pos, vel, acc, jerk, elapsed, masses, active, listing, count, in_sem,
    src, tgt, spread, far, near, flags, out_tx, out_rx,
    src_send, src_recv, tgt_send, tgt_recv, out_send, out_recv,
):
    blk, grp = lax.axis_index("blk"), lax.axis_index("grp")
    res_dev = pos.shape[1]
    act_dev = active.shape[1]
    blk_dev = res_dev // BLOCK
    per_pack = LANES // act_dev
    packs = n_blk // per_pack

    barrier = pltpu.get_barrier_semaphore()
    for k in range(1, n_grp):
        pl.semaphore_signal(
            barrier, inc=1, device_id=(blk, xor(grp, k, n_grp)), device_id_type=MESH
        )
    for k in range(1, n_blk):
        pl.semaphore_signal(
            barrier, inc=1, device_id=(xor(blk, k, n_blk), grp), device_id_type=MESH
        )

    loads = [
        pltpu.make_async_copy(there, here, in_sem.at[i])
        for i, (there, here) in enumerate(
            (
                (pos_hbm, pos), (vel_hbm, vel), (acc_hbm, acc), (jerk_hbm, jerk),
                (elapsed_hbm, elapsed), (masses_hbm, masses), (active_hbm, active),
                (listing_hbm, listing), (count_hbm, count),
            )
        )
    ]
    for load in loads:
        load.start()
    for load in loads:
        load.wait()
    t = elapsed[...]
    p, v, a, j = pos[...], vel[...], acc[...], jerk[...]
    src[0, 0:3, :] = p + t * (v + t * (0.5 * a + t * j / 6.0))
    src[0, 3:6, :] = v + t * (a + 0.5 * t * j)
    src[0, 6:7, :] = masses[...]
    src[0, 7:8, :] = t

    chosen = jnp.concatenate([active[...]] * per_pack, axis=1)
    chosen = jnp.broadcast_to(chosen, (8, LANES))
    place = chosen % BLOCK
    old = jnp.concatenate([a, j, t, t], axis=0)
    own_new = jnp.zeros((8, LANES), jnp.float32)
    own_old = jnp.zeros((8, LANES), jnp.float32)
    for b in range(blk_dev):
        here = chosen // BLOCK == b
        cut = slice(b * BLOCK, (b + 1) * BLOCK)
        own_new = jnp.where(
            here, jnp.take_along_axis(src[0, :, cut], place, axis=1), own_new
        )
        own_old = jnp.where(
            here, jnp.take_along_axis(old[:, cut], place, axis=1), own_old
        )
    tgt[0] = own_new
    far[...] = jnp.zeros_like(far)
    near[...] = jnp.zeros_like(near)

    pl.semaphore_wait(barrier, n_grp - 1 + n_blk - 1)

    def tgt_copy(k):
        return pltpu.make_async_remote_copy(
            src_ref=tgt.at[0], dst_ref=tgt.at[k],
            send_sem=tgt_send.at[k], recv_sem=tgt_recv.at[k],
            device_id=(xor(blk, k, n_blk), grp), device_id_type=MESH,
        )

    def src_copy(k):
        return pltpu.make_async_remote_copy(
            src_ref=src.at[0], dst_ref=src.at[k],
            send_sem=src_send.at[k], recv_sem=src_recv.at[k],
            device_id=(blk, xor(grp, k, n_grp)), device_id_type=MESH,
        )

    def out_copy(k):
        pack = k // per_pack
        return pltpu.make_async_remote_copy(
            src_ref=out_tx.at[pack], dst_ref=out_rx.at[k],
            send_sem=out_send.at[k], recv_sem=out_recv.at[k],
            device_id=(xor(blk, k, n_blk), grp), device_id_type=MESH,
        )

    for k in range(1, n_blk):
        tgt_copy(k).start()
    for k in reversed(range(1, n_grp)):
        src_copy(k).start()

    slots = listing.shape[1]
    names = lax.broadcasted_iota(jnp.int32, (blk_dev * n_grp, slots), 0)
    spots = lax.broadcasted_iota(jnp.int32, (blk_dev * n_grp, slots), 1)
    hit = (listing[...] == names) & (spots < count[0])
    member = jnp.max(jnp.where(hit, 1.0, 0.0), axis=1, keepdims=True)
    flags[...] = jnp.broadcast_to(member, flags.shape)

    for k in range(1, n_blk):
        tgt_copy(k).wait_recv()
    lane = lax.broadcasted_iota(jnp.int32, (8, LANES), 1)
    for pack in range(packs):
        mixed = tgt[pack * per_pack]
        for i in range(1, per_pack):
            mixed = jnp.where(lane >= i * act_dev, tgt[pack * per_pack + i], mixed)
        turned = mixed.T
        for c in range(6):
            spread[c, pack * LANES : (pack + 1) * LANES, :] = jnp.broadcast_to(
                turned[:, c : c + 1], (LANES, LANES)
            )

    def block_slot(i):
        before = i - 1
        other = before + (before + n_grp - grp) // n_grp
        return jnp.where(i == 0, 0, xor(grp, other, n_grp))

    def source_rows(k):
        return [
            [src[k, c : c + 1, b * BLOCK : (b + 1) * BLOCK] for c in range(7)]
            for b in range(blk_dev)
        ]

    def add_others(i, carry):
        k = block_slot(i)

        @pl.when(i > 0)
        def _():
            src_copy(k).wait_recv()

        source = source_rows(k)
        for slot in range(1, n_blk):
            rows = slice(slot * act_dev, (slot + 1) * act_dev)
            target = [spread[c, rows, :] for c in range(6)]
            terms = pair_terms(target, source[0])
            for b in range(1, blk_dev):
                terms = [x + y for x, y in zip(terms, pair_terms(target, source[b]))]
            for c in range(6):
                far[c, rows, :] = far[c, rows, :] + terms[c]
        return carry

    lax.fori_loop(0, n_grp, add_others, 0)

    lanes = lax.broadcasted_iota(jnp.int32, (LANES, LANES), 1)
    for pack in range(packs):
        rows = slice(pack * LANES, (pack + 1) * LANES)
        packed = jnp.zeros((LANES, LANES), jnp.float32)
        for c in range(6):
            total = jnp.sum(far[c, rows, :], axis=1, keepdims=True)
            packed = jnp.where(lanes == c, total, packed)
        out_tx[pack] = packed.T[0:8, :]
        for k in range(max(1, pack * per_pack), (pack + 1) * per_pack):
            out_copy(k).start()

    own = slice(0, act_dev)

    def add_own(i, carry):
        target = [spread[c, own, :] for c in range(6)]
        far_sum = [far[c, own, :] for c in range(6)]
        near_sum = [near[c] for c in range(6)]
        for k in (2 * i, 2 * i + 1):
            source = source_rows(k)
            for b in range(blk_dev):
                block_id = xor(grp, k, n_grp) * blk_dev + b
                is_near = flags[pl.ds(block_id, 1), :]
                for c, term in enumerate(pair_terms(target, source[b])):
                    kept = term * is_near
                    near_sum[c] = near_sum[c] + kept
                    far_sum[c] = far_sum[c] + (term - kept)
        for c in range(6):
            far[c, own, :] = far_sum[c]
            near[c] = near_sum[c]
        return carry

    lax.fori_loop(0, n_grp // 2, add_own, 0)

    packed = jnp.zeros((act_dev, LANES), jnp.float32)
    for c in range(6):
        total = jnp.sum(far[c, own, :], axis=1, keepdims=True)
        packed = jnp.where(lanes[:act_dev] == c, total, packed)
        total = jnp.sum(near[c], axis=1, keepdims=True)
        packed = jnp.where(lanes[:act_dev] == c + 8, total, packed)
    flat = packed.T
    reg, irr = flat[0:6, :], flat[8:14, :]

    result[8:14, 0:act_dev] = irr
    for k in range(1, n_blk):
        out_copy(k).wait_recv()
        left = (k % per_pack) * act_dev
        reg = reg + out_rx[k][0:6, left : left + act_dev]
    result[0:6, 0:act_dev] = reg
    total = reg + irr
    accel_now, jerk_now = total[0:3], total[3:6]
    mine = own_old[:, 0:act_dev]
    start_accel, start_jerk, step = mine[0:3], mine[3:6], mine[6:7]
    change = start_accel - accel_now
    result[16:19, 0:act_dev] = -6.0 * change - step * (4.0 * start_jerk + 2.0 * jerk_now)
    result[19:22, 0:act_dev] = 12.0 * change + 6.0 * step * (start_jerk + jerk_now)

    for k in range(1, n_blk):
        tgt_copy(k).wait_send()
        out_copy(k).wait_send()
    for k in range(1, n_grp):
        src_copy(k).wait_send()


def write_out(result, regular, irregular, correction):
    act_dev = regular.shape[1]
    regular[...] = result[0:6, 0:act_dev]
    irregular[...] = result[8:14, 0:act_dev]
    correction[...] = result[16:22, 0:act_dev]


def per_device(
    n_blk, n_grp,
    position, velocity, accel_old, jerk_old, elapsed, masses,
    active_stars, neighbour_list, neighbour_count,
):
    act_dev = active_stars.shape[0]
    res_dev = position.shape[1]
    packs = n_blk * act_dev // LANES
    shape = jax.ShapeDtypeStruct((6, act_dev), jnp.float32)
    vmem = pl.BlockSpec(memory_space=pltpu.VMEM)
    f32 = jnp.float32
    result = pl.pallas_call(
        functools.partial(kernel, n_blk, n_grp),
        out_shape=pltpu.VMEM((24, LANES), f32),
        in_specs=[pl.BlockSpec(memory_space=pltpu.HBM)] * 9,
        out_specs=vmem,
        scratch_shapes=[
            pltpu.VMEM(position.shape, f32),
            pltpu.VMEM(position.shape, f32),
            pltpu.VMEM(position.shape, f32),
            pltpu.VMEM(position.shape, f32),
            pltpu.VMEM((1, res_dev), f32),
            pltpu.VMEM((1, res_dev), f32),
            pltpu.VMEM((1, act_dev), jnp.int32),
            pltpu.VMEM(neighbour_list.shape, jnp.int32),
            pltpu.SMEM((1,), jnp.int32),
            pltpu.SemaphoreType.DMA((9,)),
            pltpu.VMEM((n_grp, 8, res_dev), f32),
            pltpu.VMEM((n_blk, 8, LANES), f32),
            pltpu.VMEM((6, packs * LANES, LANES), f32),
            pltpu.VMEM((6, packs * LANES, LANES), f32),
            pltpu.VMEM((6, act_dev, LANES), f32),
            pltpu.VMEM((n_grp * res_dev // BLOCK, LANES), f32),
            pltpu.VMEM((packs, 8, LANES), f32),
            pltpu.VMEM((n_blk, 8, LANES), f32),
            pltpu.SemaphoreType.DMA((n_grp,)),
            pltpu.SemaphoreType.DMA((n_grp,)),
            pltpu.SemaphoreType.DMA((n_blk,)),
            pltpu.SemaphoreType.DMA((n_blk,)),
            pltpu.SemaphoreType.DMA((n_blk,)),
            pltpu.SemaphoreType.DMA((n_blk,)),
        ],
        compiler_params=pltpu.CompilerParams(collective_id=0, has_side_effects=True),
        cost_estimate=pl.CostEstimate(
            flops=40 * n_blk * act_dev * n_grp * res_dev,
            bytes_accessed=32 * res_dev * n_grp,
            transcendentals=n_blk * act_dev * n_grp * res_dev,
        ),
    )(
        position, velocity, accel_old, jerk_old,
        elapsed.reshape(1, -1), masses.reshape(1, -1), active_stars.reshape(1, -1),
        neighbour_list, neighbour_count,
    )
    return pl.pallas_call(
        write_out,
        out_shape=(shape, shape, shape),
        in_specs=[vmem],
        out_specs=(vmem, vmem, vmem),
    )(pltpu.with_memory_space_constraint(result, pltpu.VMEM))


def solution(mesh):
    stars = P(None, ("blk", "grp"))
    flat = P(("blk", "grp"))
    return jax.shard_map(
        functools.partial(per_device, mesh.shape["blk"], mesh.shape["grp"]),
        mesh=mesh,
        in_specs=(stars,) * 4 + (flat,) * 3 + (P(("blk", "grp"), None), flat),
        out_specs=(stars,) * 3,
        check_vma=False,
    )
```

```python
import functools

import jax
import jax.numpy as jnp
from jax import lax
from jax.experimental import pallas as pl
from jax.experimental.pallas import tpu as pltpu
from jax.sharding import PartitionSpec as P

BLOCK = 128
LANES = 128
SOFTEN_SQ = 0.0001
MESH = pl.DeviceIdType.MESH


def xor(a, b, size):
    out, bit = 0, 1
    while bit < size:
        out = out + ((a // bit + b // bit) % 2) * bit
        bit *= 2
    return out


def pair_terms(target, source):
    gap = [source[c] - target[c] for c in range(3)]
    rel = [source[c + 3] - target[c + 3] for c in range(3)]
    dist_sq = gap[0] * gap[0] + gap[1] * gap[1] + gap[2] * gap[2] + SOFTEN_SQ
    inverse = lax.rsqrt(dist_sq)
    inv_sq = inverse * inverse
    scaled = source[6] * (inv_sq * inverse)
    radial = (gap[0] * rel[0] + gap[1] * rel[1] + gap[2] * rel[2]) * (3.0 * inv_sq)
    return [scaled * g for g in gap] + [
        scaled * (r - radial * g) for r, g in zip(rel, gap)
    ]


def kernel(
    n_blk, n_grp,
    pos_hbm, vel_hbm, acc_hbm, jerk_hbm, elapsed_hbm, masses_hbm, active_hbm,
    listing_hbm, count_hbm, result,
    pos, vel, acc, jerk, elapsed, masses, active, listing, count, in_sem,
    src, tgt, spread, far, near, flags, out_tx, out_rx,
    src_send, src_recv, tgt_send, tgt_recv, out_send, out_recv,
):
    blk, grp = lax.axis_index("blk"), lax.axis_index("grp")
    res_dev = pos.shape[1]
    act_dev = active.shape[1]
    blk_dev = res_dev // BLOCK
    per_pack = LANES // act_dev
    packs = n_blk // per_pack

    barrier = pltpu.get_barrier_semaphore()
    for k in [1, *range(2, n_grp, 2)]:
        pl.semaphore_signal(
            barrier, inc=1, device_id=(blk, xor(grp, k, n_grp)), device_id_type=MESH
        )
    for k in range(1, n_blk):
        pl.semaphore_signal(
            barrier, inc=1, device_id=(xor(blk, k, n_blk), grp), device_id_type=MESH
        )

    loads = [
        pltpu.make_async_copy(there, here, in_sem.at[i])
        for i, (there, here) in enumerate(
            (
                (pos_hbm, pos), (vel_hbm, vel), (acc_hbm, acc), (jerk_hbm, jerk),
                (elapsed_hbm, elapsed), (masses_hbm, masses), (active_hbm, active),
                (listing_hbm, listing), (count_hbm, count),
            )
        )
    ]
    for load in loads:
        load.start()
    for load in loads:
        load.wait()
    t = elapsed[...]
    p, v, a, j = pos[...], vel[...], acc[...], jerk[...]
    src[0, 0:3, :] = p + t * (v + t * (0.5 * a + t * j / 6.0))
    src[0, 3:6, :] = v + t * (a + 0.5 * t * j)
    src[0, 6:7, :] = masses[...]
    src[0, 7:8, :] = t

    chosen = jnp.concatenate([active[...]] * per_pack, axis=1)
    chosen = jnp.broadcast_to(chosen, (8, LANES))
    place = chosen % BLOCK
    old = jnp.concatenate([a, j, t, t], axis=0)
    own_new = jnp.zeros((8, LANES), jnp.float32)
    own_old = jnp.zeros((8, LANES), jnp.float32)
    for b in range(blk_dev):
        here = chosen // BLOCK == b
        cut = slice(b * BLOCK, (b + 1) * BLOCK)
        own_new = jnp.where(
            here, jnp.take_along_axis(src[0, :, cut], place, axis=1), own_new
        )
        own_old = jnp.where(
            here, jnp.take_along_axis(old[:, cut], place, axis=1), own_old
        )
    tgt[0] = own_new
    far[...] = jnp.zeros_like(far)
    near[...] = jnp.zeros_like(near)

    pl.semaphore_wait(barrier, n_grp // 2 + n_blk - 1)

    def tgt_copy(k):
        return pltpu.make_async_remote_copy(
            src_ref=tgt.at[0], dst_ref=tgt.at[k],
            send_sem=tgt_send.at[k], recv_sem=tgt_recv.at[k],
            device_id=(xor(blk, k, n_blk), grp), device_id_type=MESH,
        )

    def src_copy(k):
        return pltpu.make_async_remote_copy(
            src_ref=src.at[0], dst_ref=src.at[k],
            send_sem=src_send.at[k], recv_sem=src_recv.at[k],
            device_id=(blk, xor(grp, k, n_grp)), device_id_type=MESH,
        )

    def hand_on(k):
        return pltpu.make_async_remote_copy(
            src_ref=src.at[k], dst_ref=src.at[k + 1],
            send_sem=src_send.at[k + 1], recv_sem=src_recv.at[k + 1],
            device_id=(blk, xor(grp, 1, n_grp)), device_id_type=MESH,
        )

    def out_copy(k):
        pack = k // per_pack
        return pltpu.make_async_remote_copy(
            src_ref=out_tx.at[pack], dst_ref=out_rx.at[k],
            send_sem=out_send.at[k], recv_sem=out_recv.at[k],
            device_id=(xor(blk, k, n_blk), grp), device_id_type=MESH,
        )

    for k in range(1, n_blk):
        tgt_copy(k).start()
    for k in reversed(range(2, n_grp, 2)):
        src_copy(k).start()
    hand_on(0).start()

    slots = listing.shape[1]
    names = lax.broadcasted_iota(jnp.int32, (blk_dev * n_grp, slots), 0)
    spots = lax.broadcasted_iota(jnp.int32, (blk_dev * n_grp, slots), 1)
    hit = (listing[...] == names) & (spots < count[0])
    member = jnp.max(jnp.where(hit, 1.0, 0.0), axis=1, keepdims=True)
    flags[...] = jnp.broadcast_to(member, flags.shape)

    for k in range(1, n_blk):
        tgt_copy(k).wait_recv()
    lane = lax.broadcasted_iota(jnp.int32, (8, LANES), 1)
    for pack in range(packs):
        mixed = tgt[pack * per_pack]
        for i in range(1, per_pack):
            mixed = jnp.where(lane >= i * act_dev, tgt[pack * per_pack + i], mixed)
        turned = mixed.T
        for c in range(6):
            spread[c, pack * LANES : (pack + 1) * LANES, :] = jnp.broadcast_to(
                turned[:, c : c + 1], (LANES, LANES)
            )

    def source_rows(k):
        return [
            [
                jnp.broadcast_to(
                    src[k, c : c + 1, b * BLOCK : (b + 1) * BLOCK], (8, LANES)
                )
                for c in range(7)
            ]
            for b in range(blk_dev)
        ]

    def add_others(k):
        source = source_rows(k)
        for low in range(act_dev, n_blk * act_dev, 8):
            rows = slice(low, low + 8)
            target = [spread[c, rows, :] for c in range(6)]
            terms = pair_terms(target, source[0])
            for b in range(1, blk_dev):
                terms = [x + y for x, y in zip(terms, pair_terms(target, source[b]))]
            for c in range(6):
                far[c, rows, :] = far[c, rows, :] + terms[c]

    def two_devices(i, carry):
        k = 2 * i

        @pl.when(i > 0)
        def _():
            src_copy(k).wait_recv()
            hand_on(k).start()

        add_others(k)
        hand_on(k).wait_recv()
        add_others(k + 1)
        return carry

    lax.fori_loop(0, n_grp // 2, two_devices, 0)

    lanes = lax.broadcasted_iota(jnp.int32, (LANES, LANES), 1)
    for pack in range(packs):
        rows = slice(pack * LANES, (pack + 1) * LANES)
        packed = jnp.zeros((LANES, LANES), jnp.float32)
        for c in range(6):
            total = jnp.sum(far[c, rows, :], axis=1, keepdims=True)
            packed = jnp.where(lanes == c, total, packed)
        out_tx[pack] = packed.T[0:8, :]
        for k in range(max(1, pack * per_pack), (pack + 1) * per_pack):
            out_copy(k).start()

    own = slice(0, act_dev)

    def add_own(k, carry):
        source = source_rows(k)
        is_near = []
        for b in range(blk_dev):
            block_id = xor(grp, k, n_grp) * blk_dev + b
            is_near.append(jnp.broadcast_to(flags[pl.ds(block_id, 1), :], (8, LANES)))
        for low in range(0, act_dev, 8):
            rows = slice(low, low + 8)
            target = [spread[c, rows, :] for c in range(6)]
            far_sum = [far[c, rows, :] for c in range(6)]
            near_sum = [near[c, rows, :] for c in range(6)]
            for b in range(blk_dev):
                for c, term in enumerate(pair_terms(target, source[b])):
                    kept = term * is_near[b]
                    near_sum[c] = near_sum[c] + kept
                    far_sum[c] = far_sum[c] + (term - kept)
            for c in range(6):
                far[c, rows, :] = far_sum[c]
                near[c, rows, :] = near_sum[c]
        return carry

    lax.fori_loop(0, n_grp, add_own, 0)

    packed = jnp.zeros((act_dev, LANES), jnp.float32)
    for c in range(6):
        total = jnp.sum(far[c, own, :], axis=1, keepdims=True)
        packed = jnp.where(lanes[:act_dev] == c, total, packed)
        total = jnp.sum(near[c], axis=1, keepdims=True)
        packed = jnp.where(lanes[:act_dev] == c + 8, total, packed)
    flat = packed.T
    reg, irr = flat[0:6, :], flat[8:14, :]

    result[8:14, 0:act_dev] = irr
    for k in range(1, n_blk):
        out_copy(k).wait_recv()
        left = (k % per_pack) * act_dev
        reg = reg + out_rx[k][0:6, left : left + act_dev]
    result[0:6, 0:act_dev] = reg
    total = reg + irr
    accel_now, jerk_now = total[0:3], total[3:6]
    mine = own_old[:, 0:act_dev]
    start_accel, start_jerk, step = mine[0:3], mine[3:6], mine[6:7]
    change = start_accel - accel_now
    result[16:19, 0:act_dev] = -6.0 * change - step * (4.0 * start_jerk + 2.0 * jerk_now)
    result[19:22, 0:act_dev] = 12.0 * change + 6.0 * step * (start_jerk + jerk_now)

    for k in range(1, n_blk):
        tgt_copy(k).wait_send()
        out_copy(k).wait_send()
    for k in range(0, n_grp, 2):
        hand_on(k).wait_send()
    for k in range(2, n_grp, 2):
        src_copy(k).wait_send()


def write_out(result, regular, irregular, correction):
    act_dev = regular.shape[1]
    regular[...] = result[0:6, 0:act_dev]
    irregular[...] = result[8:14, 0:act_dev]
    correction[...] = result[16:22, 0:act_dev]


def per_device(
    n_blk, n_grp,
    position, velocity, accel_old, jerk_old, elapsed, masses,
    active_stars, neighbour_list, neighbour_count,
):
    act_dev = active_stars.shape[0]
    res_dev = position.shape[1]
    packs = n_blk * act_dev // LANES
    shape = jax.ShapeDtypeStruct((6, act_dev), jnp.float32)
    vmem = pl.BlockSpec(memory_space=pltpu.VMEM)
    f32 = jnp.float32
    result = pl.pallas_call(
        functools.partial(kernel, n_blk, n_grp),
        out_shape=pltpu.VMEM((24, LANES), f32),
        in_specs=[pl.BlockSpec(memory_space=pltpu.HBM)] * 9,
        out_specs=vmem,
        scratch_shapes=[
            pltpu.VMEM(position.shape, f32),
            pltpu.VMEM(position.shape, f32),
            pltpu.VMEM(position.shape, f32),
            pltpu.VMEM(position.shape, f32),
            pltpu.VMEM((1, res_dev), f32),
            pltpu.VMEM((1, res_dev), f32),
            pltpu.VMEM((1, act_dev), jnp.int32),
            pltpu.VMEM(neighbour_list.shape, jnp.int32),
            pltpu.SMEM((1,), jnp.int32),
            pltpu.SemaphoreType.DMA((9,)),
            pltpu.VMEM((n_grp, 8, res_dev), f32),
            pltpu.VMEM((n_blk, 8, LANES), f32),
            pltpu.VMEM((6, packs * LANES, LANES), f32),
            pltpu.VMEM((6, packs * LANES, LANES), f32),
            pltpu.VMEM((6, act_dev, LANES), f32),
            pltpu.VMEM((n_grp * res_dev // BLOCK, LANES), f32),
            pltpu.VMEM((packs, 8, LANES), f32),
            pltpu.VMEM((n_blk, 8, LANES), f32),
            pltpu.SemaphoreType.DMA((n_grp,)),
            pltpu.SemaphoreType.DMA((n_grp,)),
            pltpu.SemaphoreType.DMA((n_blk,)),
            pltpu.SemaphoreType.DMA((n_blk,)),
            pltpu.SemaphoreType.DMA((n_blk,)),
            pltpu.SemaphoreType.DMA((n_blk,)),
        ],
        compiler_params=pltpu.CompilerParams(collective_id=0, has_side_effects=True),
        cost_estimate=pl.CostEstimate(
            flops=40 * n_blk * act_dev * n_grp * res_dev,
            bytes_accessed=32 * res_dev * n_grp,
            transcendentals=n_blk * act_dev * n_grp * res_dev,
        ),
    )(
        position, velocity, accel_old, jerk_old,
        elapsed.reshape(1, -1), masses.reshape(1, -1), active_stars.reshape(1, -1),
        neighbour_list, neighbour_count,
    )
    return pl.pallas_call(
        write_out,
        out_shape=(shape, shape, shape),
        in_specs=[vmem],
        out_specs=(vmem, vmem, vmem),
    )(pltpu.with_memory_space_constraint(result, pltpu.VMEM))


def solution(mesh):
    stars = P(None, ("blk", "grp"))
    flat = P(("blk", "grp"))
    return jax.shard_map(
        functools.partial(per_device, mesh.shape["blk"], mesh.shape["grp"]),
        mesh=mesh,
        in_specs=(stars,) * 4 + (flat,) * 3 + (P(("blk", "grp"), None), flat),
        out_specs=(stars,) * 3,
        check_vma=False,
    )
```

```python
import functools

import jax
import jax.numpy as jnp
from jax import lax
from jax.experimental import pallas as pl
from jax.experimental.pallas import tpu as pltpu
from jax.sharding import PartitionSpec as P

BLOCK = 128
LANES = 128
SOFTEN_SQ = 0.0001
MESH = pl.DeviceIdType.MESH


def xor(a, b, size):
    out, bit = 0, 1
    while bit < size:
        out = out + ((a // bit + b // bit) % 2) * bit
        bit *= 2
    return out


def pair_terms(target, source):
    gap = [source[c] - target[c] for c in range(3)]
    rel = [source[c + 3] - target[c + 3] for c in range(3)]
    dist_sq = gap[0] * gap[0] + gap[1] * gap[1] + gap[2] * gap[2] + SOFTEN_SQ
    inverse = lax.rsqrt(dist_sq)
    inv_sq = inverse * inverse
    scaled = source[6] * (inv_sq * inverse)
    radial = (gap[0] * rel[0] + gap[1] * rel[1] + gap[2] * rel[2]) * (3.0 * inv_sq)
    return [scaled * g for g in gap] + [
        scaled * (r - radial * g) for r, g in zip(rel, gap)
    ]


def kernel(
    n_blk, n_grp,
    pos_hbm, vel_hbm, acc_hbm, jerk_hbm, elapsed_hbm, masses_hbm, active_hbm,
    listing_hbm, count_hbm, result,
    pos, vel, acc, jerk, elapsed, masses, active, listing, count, in_sem,
    src, tgt, spread, far, near, flags, out_tx, out_rx,
    src_send, src_recv, tgt_send, tgt_recv, out_send, out_recv,
):
    blk, grp = lax.axis_index("blk"), lax.axis_index("grp")
    res_dev = pos.shape[1]
    act_dev = active.shape[1]
    blk_dev = res_dev // BLOCK
    per_pack = LANES // act_dev
    packs = n_blk // per_pack

    barrier = pltpu.get_barrier_semaphore()
    for k in [1, *range(2, n_grp, 2)]:
        pl.semaphore_signal(
            barrier, inc=1, device_id=(blk, xor(grp, k, n_grp)), device_id_type=MESH
        )
    for k in range(1, n_blk):
        pl.semaphore_signal(
            barrier, inc=1, device_id=(xor(blk, k, n_blk), grp), device_id_type=MESH
        )

    loads = [
        pltpu.make_async_copy(there, here, in_sem.at[i])
        for i, (there, here) in enumerate(
            (
                (pos_hbm, pos), (vel_hbm, vel), (acc_hbm, acc), (jerk_hbm, jerk),
                (elapsed_hbm, elapsed), (masses_hbm, masses), (active_hbm, active),
                (listing_hbm, listing), (count_hbm, count),
            )
        )
    ]
    for load in loads:
        load.start()
    for load in loads:
        load.wait()
    t = elapsed[...]
    p, v, a, j = pos[...], vel[...], acc[...], jerk[...]
    src[0, 0:3, :] = p + t * (v + t * (0.5 * a + t * j / 6.0))
    src[0, 3:6, :] = v + t * (a + 0.5 * t * j)
    src[0, 6:7, :] = masses[...]
    src[0, 7:8, :] = t

    chosen = jnp.concatenate([active[...]] * per_pack, axis=1)
    chosen = jnp.broadcast_to(chosen, (8, LANES))
    place = chosen % BLOCK
    old = jnp.concatenate([a, j, t, t], axis=0)
    own_new = jnp.zeros((8, LANES), jnp.float32)
    own_old = jnp.zeros((8, LANES), jnp.float32)
    for b in range(blk_dev):
        here = chosen // BLOCK == b
        cut = slice(b * BLOCK, (b + 1) * BLOCK)
        own_new = jnp.where(
            here, jnp.take_along_axis(src[0, :, cut], place, axis=1), own_new
        )
        own_old = jnp.where(
            here, jnp.take_along_axis(old[:, cut], place, axis=1), own_old
        )
    tgt[0] = own_new
    far[...] = jnp.zeros_like(far)
    near[...] = jnp.zeros_like(near)

    pl.semaphore_wait(barrier, n_grp // 2 + n_blk - 1)

    def tgt_copy(k):
        return pltpu.make_async_remote_copy(
            src_ref=tgt.at[0], dst_ref=tgt.at[k],
            send_sem=tgt_send.at[k], recv_sem=tgt_recv.at[k],
            device_id=(xor(blk, k, n_blk), grp), device_id_type=MESH,
        )

    def src_copy(k):
        return pltpu.make_async_remote_copy(
            src_ref=src.at[0], dst_ref=src.at[k],
            send_sem=src_send.at[k], recv_sem=src_recv.at[k],
            device_id=(blk, xor(grp, k, n_grp)), device_id_type=MESH,
        )

    def hand_on(k):
        return pltpu.make_async_remote_copy(
            src_ref=src.at[k], dst_ref=src.at[k + 1],
            send_sem=src_send.at[k + 1], recv_sem=src_recv.at[k + 1],
            device_id=(blk, xor(grp, 1, n_grp)), device_id_type=MESH,
        )

    def out_copy(k):
        pack = k // per_pack
        return pltpu.make_async_remote_copy(
            src_ref=out_tx.at[pack], dst_ref=out_rx.at[k],
            send_sem=out_send.at[k], recv_sem=out_recv.at[k],
            device_id=(xor(blk, k, n_blk), grp), device_id_type=MESH,
        )

    for k in range(1, n_blk):
        tgt_copy(k).start()
    for k in reversed(range(2, n_grp, 2)):
        src_copy(k).start()
    hand_on(0).start()

    slots = listing.shape[1]
    names = lax.broadcasted_iota(jnp.int32, (blk_dev * n_grp, slots), 0)
    spots = lax.broadcasted_iota(jnp.int32, (blk_dev * n_grp, slots), 1)
    hit = (listing[...] == names) & (spots < count[0])
    member = jnp.max(jnp.where(hit, 1.0, 0.0), axis=1, keepdims=True)
    flags[...] = jnp.broadcast_to(member, flags.shape)

    for k in range(1, n_blk):
        tgt_copy(k).wait_recv()
    lane = lax.broadcasted_iota(jnp.int32, (8, LANES), 1)
    for pack in range(packs):
        mixed = tgt[pack * per_pack]
        for i in range(1, per_pack):
            mixed = jnp.where(lane >= i * act_dev, tgt[pack * per_pack + i], mixed)
        turned = mixed.T
        for c in range(6):
            spread[c, pack * LANES : (pack + 1) * LANES, :] = jnp.broadcast_to(
                turned[:, c : c + 1], (LANES, LANES)
            )

    def source_rows(k):
        return [
            [
                jnp.broadcast_to(
                    src[k, c : c + 1, b * BLOCK : (b + 1) * BLOCK], (act_dev, LANES)
                )
                for c in range(7)
            ]
            for b in range(blk_dev)
        ]

    def add_others(k):
        source = source_rows(k)
        for low in range(act_dev, n_blk * act_dev, act_dev):
            rows = slice(low, low + act_dev)
            target = [spread[c, rows, :] for c in range(6)]
            terms = pair_terms(target, source[0])
            for b in range(1, blk_dev):
                terms = [x + y for x, y in zip(terms, pair_terms(target, source[b]))]
            for c in range(6):
                far[c, rows, :] = far[c, rows, :] + terms[c]

    def two_devices(i, carry):
        k = 2 * i

        @pl.when(i > 0)
        def _():
            src_copy(k).wait_recv()
            hand_on(k).start()

        add_others(k)
        hand_on(k).wait_recv()
        add_others(k + 1)
        return carry

    lax.fori_loop(0, n_grp // 2, two_devices, 0)

    lanes = lax.broadcasted_iota(jnp.int32, (LANES, LANES), 1)
    for pack in range(packs):
        rows = slice(pack * LANES, (pack + 1) * LANES)
        packed = jnp.zeros((LANES, LANES), jnp.float32)
        for c in range(6):
            total = jnp.sum(far[c, rows, :], axis=1, keepdims=True)
            packed = jnp.where(lanes == c, total, packed)
        out_tx[pack] = packed.T[0:8, :]
        for k in range(max(1, pack * per_pack), (pack + 1) * per_pack):
            out_copy(k).start()

    own = slice(0, act_dev)

    def add_own(k, carry):
        source = source_rows(k)
        is_near = []
        for b in range(blk_dev):
            block_id = xor(grp, k, n_grp) * blk_dev + b
            is_near.append(jnp.broadcast_to(flags[pl.ds(block_id, 1), :], (act_dev, LANES)))
        for low in range(0, act_dev, act_dev):
            rows = slice(low, low + act_dev)
            target = [spread[c, rows, :] for c in range(6)]
            far_sum = [far[c, rows, :] for c in range(6)]
            near_sum = [near[c, rows, :] for c in range(6)]
            for b in range(blk_dev):
                for c, term in enumerate(pair_terms(target, source[b])):
                    kept = term * is_near[b]
                    near_sum[c] = near_sum[c] + kept
                    far_sum[c] = far_sum[c] + (term - kept)
            for c in range(6):
                far[c, rows, :] = far_sum[c]
                near[c, rows, :] = near_sum[c]
        return carry

    lax.fori_loop(0, n_grp, add_own, 0)

    packed = jnp.zeros((act_dev, LANES), jnp.float32)
    for c in range(6):
        total = jnp.sum(far[c, own, :], axis=1, keepdims=True)
        packed = jnp.where(lanes[:act_dev] == c, total, packed)
        total = jnp.sum(near[c], axis=1, keepdims=True)
        packed = jnp.where(lanes[:act_dev] == c + 8, total, packed)
    flat = packed.T
    reg, irr = flat[0:6, :], flat[8:14, :]

    result[8:14, 0:act_dev] = irr
    for k in range(1, n_blk):
        out_copy(k).wait_recv()
        left = (k % per_pack) * act_dev
        reg = reg + out_rx[k][0:6, left : left + act_dev]
    result[0:6, 0:act_dev] = reg
    total = reg + irr
    accel_now, jerk_now = total[0:3], total[3:6]
    mine = own_old[:, 0:act_dev]
    start_accel, start_jerk, step = mine[0:3], mine[3:6], mine[6:7]
    change = start_accel - accel_now
    result[16:19, 0:act_dev] = -6.0 * change - step * (4.0 * start_jerk + 2.0 * jerk_now)
    result[19:22, 0:act_dev] = 12.0 * change + 6.0 * step * (start_jerk + jerk_now)

    for k in range(1, n_blk):
        tgt_copy(k).wait_send()
        out_copy(k).wait_send()
    for k in range(0, n_grp, 2):
        hand_on(k).wait_send()
    for k in range(2, n_grp, 2):
        src_copy(k).wait_send()


def write_out(result, regular, irregular, correction):
    act_dev = regular.shape[1]
    regular[...] = result[0:6, 0:act_dev]
    irregular[...] = result[8:14, 0:act_dev]
    correction[...] = result[16:22, 0:act_dev]


def per_device(
    n_blk, n_grp,
    position, velocity, accel_old, jerk_old, elapsed, masses,
    active_stars, neighbour_list, neighbour_count,
):
    act_dev = active_stars.shape[0]
    res_dev = position.shape[1]
    packs = n_blk * act_dev // LANES
    shape = jax.ShapeDtypeStruct((6, act_dev), jnp.float32)
    vmem = pl.BlockSpec(memory_space=pltpu.VMEM)
    f32 = jnp.float32
    result = pl.pallas_call(
        functools.partial(kernel, n_blk, n_grp),
        out_shape=pltpu.VMEM((24, LANES), f32),
        in_specs=[pl.BlockSpec(memory_space=pltpu.HBM)] * 9,
        out_specs=vmem,
        scratch_shapes=[
            pltpu.VMEM(position.shape, f32),
            pltpu.VMEM(position.shape, f32),
            pltpu.VMEM(position.shape, f32),
            pltpu.VMEM(position.shape, f32),
            pltpu.VMEM((1, res_dev), f32),
            pltpu.VMEM((1, res_dev), f32),
            pltpu.VMEM((1, act_dev), jnp.int32),
            pltpu.VMEM(neighbour_list.shape, jnp.int32),
            pltpu.SMEM((1,), jnp.int32),
            pltpu.SemaphoreType.DMA((9,)),
            pltpu.VMEM((n_grp, 8, res_dev), f32),
            pltpu.VMEM((n_blk, 8, LANES), f32),
            pltpu.VMEM((6, packs * LANES, LANES), f32),
            pltpu.VMEM((6, packs * LANES, LANES), f32),
            pltpu.VMEM((6, act_dev, LANES), f32),
            pltpu.VMEM((n_grp * res_dev // BLOCK, LANES), f32),
            pltpu.VMEM((packs, 8, LANES), f32),
            pltpu.VMEM((n_blk, 8, LANES), f32),
            pltpu.SemaphoreType.DMA((n_grp,)),
            pltpu.SemaphoreType.DMA((n_grp,)),
            pltpu.SemaphoreType.DMA((n_blk,)),
            pltpu.SemaphoreType.DMA((n_blk,)),
            pltpu.SemaphoreType.DMA((n_blk,)),
            pltpu.SemaphoreType.DMA((n_blk,)),
        ],
        compiler_params=pltpu.CompilerParams(collective_id=0, has_side_effects=True),
        cost_estimate=pl.CostEstimate(
            flops=40 * n_blk * act_dev * n_grp * res_dev,
            bytes_accessed=32 * res_dev * n_grp,
            transcendentals=n_blk * act_dev * n_grp * res_dev,
        ),
    )(
        position, velocity, accel_old, jerk_old,
        elapsed.reshape(1, -1), masses.reshape(1, -1), active_stars.reshape(1, -1),
        neighbour_list, neighbour_count,
    )
    return pl.pallas_call(
        write_out,
        out_shape=(shape, shape, shape),
        in_specs=[vmem],
        out_specs=(vmem, vmem, vmem),
    )(pltpu.with_memory_space_constraint(result, pltpu.VMEM))


def solution(mesh):
    stars = P(None, ("blk", "grp"))
    flat = P(("blk", "grp"))
    return jax.shard_map(
        functools.partial(per_device, mesh.shape["blk"], mesh.shape["grp"]),
        mesh=mesh,
        in_specs=(stars,) * 4 + (flat,) * 3 + (P(("blk", "grp"), None), flat),
        out_specs=(stars,) * 3,
        check_vma=False,
    )
```

```python
import functools

import jax
import jax.numpy as jnp
from jax import lax
from jax.experimental import pallas as pl
from jax.experimental.pallas import tpu as pltpu
from jax.sharding import PartitionSpec as P

BLOCK = 128
LANES = 128
SOFTEN_SQ = 0.0001
MESH = pl.DeviceIdType.MESH


def xor(a, b, size):
    out, bit = 0, 1
    while bit < size:
        out = out + ((a // bit + b // bit) % 2) * bit
        bit *= 2
    return out


def pair_terms(target, source):
    gap = [source[c] - target[c] for c in range(3)]
    rel = [source[c + 3] - target[c + 3] for c in range(3)]
    dist_sq = gap[0] * gap[0] + gap[1] * gap[1] + gap[2] * gap[2] + SOFTEN_SQ
    inverse = lax.rsqrt(dist_sq)
    inv_sq = inverse * inverse
    scaled = source[6] * (inv_sq * inverse)
    radial = (gap[0] * rel[0] + gap[1] * rel[1] + gap[2] * rel[2]) * (3.0 * inv_sq)
    return [scaled * g for g in gap] + [
        scaled * (r - radial * g) for r, g in zip(rel, gap)
    ]


def kernel(
    n_blk, n_grp,
    pos_hbm, vel_hbm, acc_hbm, jerk_hbm, elapsed_hbm, masses_hbm, active_hbm,
    listing_hbm, count_hbm, result,
    pos, vel, acc, jerk, elapsed, masses, active, listing, count, in_sem,
    src, tgt, spread, far, near, flags, out_tx, out_rx,
    src_send, src_recv, tgt_send, tgt_recv, out_send, out_recv,
):
    blk, grp = lax.axis_index("blk"), lax.axis_index("grp")
    res_dev = pos.shape[1]
    act_dev = active.shape[1]
    blk_dev = res_dev // BLOCK
    per_pack = LANES // act_dev
    packs = n_blk // per_pack

    barrier = pltpu.get_barrier_semaphore()
    for k in range(1, n_grp):
        pl.semaphore_signal(
            barrier, inc=1, device_id=(blk, xor(grp, k, n_grp)), device_id_type=MESH
        )
    for k in range(1, n_blk):
        pl.semaphore_signal(
            barrier, inc=1, device_id=(xor(blk, k, n_blk), grp), device_id_type=MESH
        )

    loads = [
        pltpu.make_async_copy(there, here, in_sem.at[i])
        for i, (there, here) in enumerate(
            (
                (pos_hbm, pos), (vel_hbm, vel), (acc_hbm, acc), (jerk_hbm, jerk),
                (elapsed_hbm, elapsed), (masses_hbm, masses), (active_hbm, active),
                (listing_hbm, listing), (count_hbm, count),
            )
        )
    ]
    for load in loads:
        load.start()
    for load in loads:
        load.wait()
    t = elapsed[...]
    p, v, a, j = pos[...], vel[...], acc[...], jerk[...]
    src[0, 0:3, :] = p + t * (v + t * (0.5 * a + t * j / 6.0))
    src[0, 3:6, :] = v + t * (a + 0.5 * t * j)
    src[0, 6:7, :] = masses[...]
    src[0, 7:8, :] = t

    chosen = jnp.concatenate([active[...]] * per_pack, axis=1)
    chosen = jnp.broadcast_to(chosen, (8, LANES))
    place = chosen % BLOCK
    old = jnp.concatenate([a, j, t, t], axis=0)
    own_new = jnp.zeros((8, LANES), jnp.float32)
    own_old = jnp.zeros((8, LANES), jnp.float32)
    for b in range(blk_dev):
        here = chosen // BLOCK == b
        cut = slice(b * BLOCK, (b + 1) * BLOCK)
        own_new = jnp.where(
            here, jnp.take_along_axis(src[0, :, cut], place, axis=1), own_new
        )
        own_old = jnp.where(
            here, jnp.take_along_axis(old[:, cut], place, axis=1), own_old
        )
    tgt[0] = own_new
    far[...] = jnp.zeros_like(far)
    near[...] = jnp.zeros_like(near)

    pl.semaphore_wait(barrier, n_grp - 1 + n_blk - 1)

    def tgt_copy(k):
        return pltpu.make_async_remote_copy(
            src_ref=tgt.at[0], dst_ref=tgt.at[k],
            send_sem=tgt_send.at[k], recv_sem=tgt_recv.at[k],
            device_id=(xor(blk, k, n_blk), grp), device_id_type=MESH,
        )

    def src_copy(k):
        return pltpu.make_async_remote_copy(
            src_ref=src.at[0], dst_ref=src.at[k],
            send_sem=src_send.at[k], recv_sem=src_recv.at[k],
            device_id=(blk, xor(grp, k, n_grp)), device_id_type=MESH,
        )

    def out_copy(k):
        pack = k // per_pack
        return pltpu.make_async_remote_copy(
            src_ref=out_tx.at[pack], dst_ref=out_rx.at[k],
            send_sem=out_send.at[k], recv_sem=out_recv.at[k],
            device_id=(xor(blk, k, n_blk), grp), device_id_type=MESH,
        )

    for k in range(1, n_blk):
        tgt_copy(k).start()
    for k in reversed(range(1, n_grp)):
        src_copy(k).start()

    slots = listing.shape[1]
    names = lax.broadcasted_iota(jnp.int32, (blk_dev * n_grp, slots), 0)
    spots = lax.broadcasted_iota(jnp.int32, (blk_dev * n_grp, slots), 1)
    hit = (listing[...] == names) & (spots < count[0])
    member = jnp.max(jnp.where(hit, 1.0, 0.0), axis=1, keepdims=True)
    flags[...] = jnp.broadcast_to(member, flags.shape)

    for k in range(1, n_blk):
        tgt_copy(k).wait_recv()
    lane = lax.broadcasted_iota(jnp.int32, (8, LANES), 1)
    for pack in range(packs):
        mixed = tgt[pack * per_pack]
        for i in range(1, per_pack):
            mixed = jnp.where(lane >= i * act_dev, tgt[pack * per_pack + i], mixed)
        turned = mixed.T
        for c in range(6):
            spread[c, pack * LANES : (pack + 1) * LANES, :] = jnp.broadcast_to(
                turned[:, c : c + 1], (LANES, LANES)
            )

    def source_rows(k):
        return [
            [src[k, c : c + 1, b * BLOCK : (b + 1) * BLOCK] for c in range(7)]
            for b in range(blk_dev)
        ]

    def add_others(k, carry):
        @pl.when(k > 0)
        def _():
            src_copy(k).wait_recv()

        source = source_rows(k)
        for slot in range(1, n_blk):
            rows = slice(slot * act_dev, (slot + 1) * act_dev)
            target = [spread[c, rows, :] for c in range(6)]
            terms = pair_terms(target, source[0])
            for b in range(1, blk_dev):
                terms = [x + y for x, y in zip(terms, pair_terms(target, source[b]))]
            for c in range(6):
                far[c, rows, :] = far[c, rows, :] + terms[c]
        return carry

    lax.fori_loop(0, n_grp, add_others, 0)

    lanes = lax.broadcasted_iota(jnp.int32, (LANES, LANES), 1)
    for pack in range(packs):
        rows = slice(pack * LANES, (pack + 1) * LANES)
        packed = jnp.zeros((LANES, LANES), jnp.float32)
        for c in range(6):
            total = jnp.sum(far[c, rows, :], axis=1, keepdims=True)
            packed = jnp.where(lanes == c, total, packed)
        out_tx[pack] = packed.T[0:8, :]
        for k in range(max(1, pack * per_pack), (pack + 1) * per_pack):
            out_copy(k).start()

    own = slice(0, act_dev)

    def add_own(i, carry):
        target = [spread[c, own, :] for c in range(6)]
        far_sum = [far[c, own, :] for c in range(6)]
        near_sum = [near[c] for c in range(6)]
        for k in (2 * i, 2 * i + 1):
            source = source_rows(k)
            for b in range(blk_dev):
                block_id = xor(grp, k, n_grp) * blk_dev + b
                is_near = flags[pl.ds(block_id, 1), :]
                for c, term in enumerate(pair_terms(target, source[b])):
                    kept = term * is_near
                    near_sum[c] = near_sum[c] + kept
                    far_sum[c] = far_sum[c] + (term - kept)
        for c in range(6):
            far[c, own, :] = far_sum[c]
            near[c] = near_sum[c]
        return carry

    lax.fori_loop(0, n_grp // 2, add_own, 0)

    packed = jnp.zeros((act_dev, LANES), jnp.float32)
    for c in range(6):
        total = jnp.sum(far[c, own, :], axis=1, keepdims=True)
        packed = jnp.where(lanes[:act_dev] == c, total, packed)
        total = jnp.sum(near[c], axis=1, keepdims=True)
        packed = jnp.where(lanes[:act_dev] == c + 8, total, packed)
    flat = packed.T
    reg, irr = flat[0:6, :], flat[8:14, :]

    result[8:14, 0:act_dev] = irr
    for k in range(1, n_blk):
        out_copy(k).wait_recv()
        left = (k % per_pack) * act_dev
        reg = reg + out_rx[k][0:6, left : left + act_dev]
    result[0:6, 0:act_dev] = reg
    total = reg + irr
    accel_now, jerk_now = total[0:3], total[3:6]
    mine = own_old[:, 0:act_dev]
    start_accel, start_jerk, step = mine[0:3], mine[3:6], mine[6:7]
    change = start_accel - accel_now
    result[16:19, 0:act_dev] = -6.0 * change - step * (4.0 * start_jerk + 2.0 * jerk_now)
    result[19:22, 0:act_dev] = 12.0 * change + 6.0 * step * (start_jerk + jerk_now)

    for k in range(1, n_blk):
        tgt_copy(k).wait_send()
        out_copy(k).wait_send()
    for k in range(1, n_grp):
        src_copy(k).wait_send()


def write_out(result, regular, irregular, correction):
    act_dev = regular.shape[1]
    regular[...] = result[0:6, 0:act_dev]
    irregular[...] = result[8:14, 0:act_dev]
    correction[...] = result[16:22, 0:act_dev]


def per_device(
    n_blk, n_grp,
    position, velocity, accel_old, jerk_old, elapsed, masses,
    active_stars, neighbour_list, neighbour_count,
):
    act_dev = active_stars.shape[0]
    res_dev = position.shape[1]
    packs = n_blk * act_dev // LANES
    shape = jax.ShapeDtypeStruct((6, act_dev), jnp.float32)
    vmem = pl.BlockSpec(memory_space=pltpu.VMEM)
    f32 = jnp.float32
    result = pl.pallas_call(
        functools.partial(kernel, n_blk, n_grp),
        out_shape=pltpu.VMEM((24, LANES), f32),
        in_specs=[pl.BlockSpec(memory_space=pltpu.HBM)] * 9,
        out_specs=vmem,
        scratch_shapes=[
            pltpu.VMEM(position.shape, f32),
            pltpu.VMEM(position.shape, f32),
            pltpu.VMEM(position.shape, f32),
            pltpu.VMEM(position.shape, f32),
            pltpu.VMEM((1, res_dev), f32),
            pltpu.VMEM((1, res_dev), f32),
            pltpu.VMEM((1, act_dev), jnp.int32),
            pltpu.VMEM(neighbour_list.shape, jnp.int32),
            pltpu.SMEM((1,), jnp.int32),
            pltpu.SemaphoreType.DMA((9,)),
            pltpu.VMEM((n_grp, 8, res_dev), f32),
            pltpu.VMEM((n_blk, 8, LANES), f32),
            pltpu.VMEM((6, packs * LANES, LANES), f32),
            pltpu.VMEM((6, packs * LANES, LANES), f32),
            pltpu.VMEM((6, act_dev, LANES), f32),
            pltpu.VMEM((n_grp * res_dev // BLOCK, LANES), f32),
            pltpu.VMEM((packs, 8, LANES), f32),
            pltpu.VMEM((n_blk, 8, LANES), f32),
            pltpu.SemaphoreType.DMA((n_grp,)),
            pltpu.SemaphoreType.DMA((n_grp,)),
            pltpu.SemaphoreType.DMA((n_blk,)),
            pltpu.SemaphoreType.DMA((n_blk,)),
            pltpu.SemaphoreType.DMA((n_blk,)),
            pltpu.SemaphoreType.DMA((n_blk,)),
        ],
        compiler_params=pltpu.CompilerParams(collective_id=0, has_side_effects=True),
        cost_estimate=pl.CostEstimate(
            flops=40 * n_blk * act_dev * n_grp * res_dev,
            bytes_accessed=32 * res_dev * n_grp,
            transcendentals=n_blk * act_dev * n_grp * res_dev,
        ),
    )(
        position, velocity, accel_old, jerk_old,
        elapsed.reshape(1, -1), masses.reshape(1, -1), active_stars.reshape(1, -1),
        neighbour_list, neighbour_count,
    )
    return pl.pallas_call(
        write_out,
        out_shape=(shape, shape, shape),
        in_specs=[vmem],
        out_specs=(vmem, vmem, vmem),
    )(pltpu.with_memory_space_constraint(result, pltpu.VMEM))


def solution(mesh):
    stars = P(None, ("blk", "grp"))
    flat = P(("blk", "grp"))
    return jax.shard_map(
        functools.partial(per_device, mesh.shape["blk"], mesh.shape["grp"]),
        mesh=mesh,
        in_specs=(stars,) * 4 + (flat,) * 3 + (P(("blk", "grp"), None), flat),
        out_specs=(stars,) * 3,
        check_vma=False,
    )
```

```python
import functools

import jax
import jax.numpy as jnp
from jax import lax
from jax.experimental import pallas as pl
from jax.experimental.pallas import tpu as pltpu
from jax.sharding import PartitionSpec as P

BLOCK = 128
LANES = 128
SOFTEN_SQ = 0.0001
MESH = pl.DeviceIdType.MESH


def xor(a, b, size):
    out, bit = 0, 1
    while bit < size:
        out = out + ((a // bit + b // bit) % 2) * bit
        bit *= 2
    return out


def pair_terms(target, source):
    gap = [source[c] - target[c] for c in range(3)]
    rel = [source[c + 3] - target[c + 3] for c in range(3)]
    dist_sq = gap[0] * gap[0] + gap[1] * gap[1] + gap[2] * gap[2] + SOFTEN_SQ
    inverse = lax.rsqrt(dist_sq)
    inv_sq = inverse * inverse
    scaled = source[6] * (inv_sq * inverse)
    radial = (gap[0] * rel[0] + gap[1] * rel[1] + gap[2] * rel[2]) * (3.0 * inv_sq)
    return [scaled * g for g in gap] + [
        scaled * (r - radial * g) for r, g in zip(rel, gap)
    ]


def kernel(
    n_blk, n_grp,
    pos_hbm, vel_hbm, acc_hbm, jerk_hbm, elapsed_hbm, masses_hbm, active_hbm,
    listing_hbm, count_hbm, result,
    pos, vel, acc, jerk, elapsed, masses, active, listing, count, in_sem,
    src, tgt, spread, far, near, flags, out_tx, out_rx,
    src_send, src_recv, tgt_send, tgt_recv, out_send, out_recv,
):
    blk, grp = lax.axis_index("blk"), lax.axis_index("grp")
    res_dev = pos.shape[1]
    act_dev = active.shape[1]
    blk_dev = res_dev // BLOCK
    per_pack = LANES // act_dev
    packs = n_blk // per_pack

    barrier = pltpu.get_barrier_semaphore()
    for k in range(1, n_grp):
        pl.semaphore_signal(
            barrier, inc=1, device_id=(blk, xor(grp, k, n_grp)), device_id_type=MESH
        )
    for k in range(1, n_blk):
        pl.semaphore_signal(
            barrier, inc=1, device_id=(xor(blk, k, n_blk), grp), device_id_type=MESH
        )

    loads = [
        pltpu.make_async_copy(there, here, in_sem.at[i])
        for i, (there, here) in enumerate(
            (
                (pos_hbm, pos), (vel_hbm, vel), (acc_hbm, acc), (jerk_hbm, jerk),
                (elapsed_hbm, elapsed), (masses_hbm, masses), (active_hbm, active),
                (listing_hbm, listing), (count_hbm, count),
            )
        )
    ]
    for load in loads:
        load.start()
    for load in loads:
        load.wait()
    t = elapsed[...]
    p, v, a, j = pos[...], vel[...], acc[...], jerk[...]
    src[0, 0:3, :] = p + t * (v + t * (0.5 * a + t * j / 6.0))
    src[0, 3:6, :] = v + t * (a + 0.5 * t * j)
    src[0, 6:7, :] = masses[...]
    src[0, 7:8, :] = t

    chosen = jnp.concatenate([active[...]] * per_pack, axis=1)
    chosen = jnp.broadcast_to(chosen, (8, LANES))
    place = chosen % BLOCK
    old = jnp.concatenate([a, j, t, t], axis=0)
    own_new = jnp.zeros((8, LANES), jnp.float32)
    own_old = jnp.zeros((8, LANES), jnp.float32)
    for b in range(blk_dev):
        here = chosen // BLOCK == b
        cut = slice(b * BLOCK, (b + 1) * BLOCK)
        own_new = jnp.where(
            here, jnp.take_along_axis(src[0, :, cut], place, axis=1), own_new
        )
        own_old = jnp.where(
            here, jnp.take_along_axis(old[:, cut], place, axis=1), own_old
        )
    tgt[0] = own_new
    far[...] = jnp.zeros_like(far)
    near[...] = jnp.zeros_like(near)

    pl.semaphore_wait(barrier, n_grp - 1 + n_blk - 1)

    def tgt_copy(k):
        return pltpu.make_async_remote_copy(
            src_ref=tgt.at[0], dst_ref=tgt.at[k],
            send_sem=tgt_send.at[k], recv_sem=tgt_recv.at[k],
            device_id=(xor(blk, k, n_blk), grp), device_id_type=MESH,
        )

    def src_copy(k):
        return pltpu.make_async_remote_copy(
            src_ref=src.at[0], dst_ref=src.at[k],
            send_sem=src_send.at[k], recv_sem=src_recv.at[k],
            device_id=(blk, xor(grp, k, n_grp)), device_id_type=MESH,
        )

    def out_copy(k):
        pack = k // per_pack
        return pltpu.make_async_remote_copy(
            src_ref=out_tx.at[pack], dst_ref=out_rx.at[k],
            send_sem=out_send.at[k], recv_sem=out_recv.at[k],
            device_id=(xor(blk, k, n_blk), grp), device_id_type=MESH,
        )

    for k in range(1, n_blk):
        tgt_copy(k).start()
    for k in range(1, n_grp):
        src_copy(k).start()

    slots = listing.shape[1]
    names = lax.broadcasted_iota(jnp.int32, (blk_dev * n_grp, slots), 0)
    spots = lax.broadcasted_iota(jnp.int32, (blk_dev * n_grp, slots), 1)
    hit = (listing[...] == names) & (spots < count[0])
    member = jnp.max(jnp.where(hit, 1.0, 0.0), axis=1, keepdims=True)
    flags[...] = jnp.broadcast_to(member, flags.shape)

    for k in range(1, n_blk):
        tgt_copy(k).wait_recv()
    lane = lax.broadcasted_iota(jnp.int32, (8, LANES), 1)
    for pack in range(packs):
        mixed = tgt[pack * per_pack]
        for i in range(1, per_pack):
            mixed = jnp.where(lane >= i * act_dev, tgt[pack * per_pack + i], mixed)
        turned = mixed.T
        for c in range(6):
            spread[c, pack * LANES : (pack + 1) * LANES, :] = jnp.broadcast_to(
                turned[:, c : c + 1], (LANES, LANES)
            )

    def source_rows(k):
        return [
            [src[k, c : c + 1, b * BLOCK : (b + 1) * BLOCK] for c in range(7)]
            for b in range(blk_dev)
        ]

    def add_others(k, carry):
        @pl.when(k > 0)
        def _():
            src_copy(k).wait_recv()

        source = source_rows(k)
        for slot in range(1, n_blk):
            rows = slice(slot * act_dev, (slot + 1) * act_dev)
            target = [spread[c, rows, :] for c in range(6)]
            terms = pair_terms(target, source[0])
            for b in range(1, blk_dev):
                terms = [x + y for x, y in zip(terms, pair_terms(target, source[b]))]
            for c in range(6):
                far[c, rows, :] = far[c, rows, :] + terms[c]
        return carry

    lax.fori_loop(0, n_grp, add_others, 0)

    lanes = lax.broadcasted_iota(jnp.int32, (LANES, LANES), 1)
    for pack in range(packs):
        rows = slice(pack * LANES, (pack + 1) * LANES)
        packed = jnp.zeros((LANES, LANES), jnp.float32)
        for c in range(6):
            total = jnp.sum(far[c, rows, :], axis=1, keepdims=True)
            packed = jnp.where(lanes == c, total, packed)
        out_tx[pack] = packed.T[0:8, :]
        for k in range(max(1, pack * per_pack), (pack + 1) * per_pack):
            out_copy(k).start()

    own = slice(0, act_dev)

    def add_own(i, carry):
        target = [spread[c, own, :] for c in range(6)]
        far_sum = [far[c, own, :] for c in range(6)]
        near_sum = [near[c] for c in range(6)]
        for k in (2 * i, 2 * i + 1):
            source = source_rows(k)
            for b in range(blk_dev):
                block_id = xor(grp, k, n_grp) * blk_dev + b
                is_near = flags[pl.ds(block_id, 1), :]
                for c, term in enumerate(pair_terms(target, source[b])):
                    kept = term * is_near
                    near_sum[c] = near_sum[c] + kept
                    far_sum[c] = far_sum[c] + (term - kept)
        for c in range(6):
            far[c, own, :] = far_sum[c]
            near[c] = near_sum[c]
        return carry

    lax.fori_loop(0, n_grp // 2, add_own, 0)

    packed = jnp.zeros((act_dev, LANES), jnp.float32)
    for c in range(6):
        total = jnp.sum(far[c, own, :], axis=1, keepdims=True)
        packed = jnp.where(lanes[:act_dev] == c, total, packed)
        total = jnp.sum(near[c], axis=1, keepdims=True)
        packed = jnp.where(lanes[:act_dev] == c + 8, total, packed)
    flat = packed.T
    reg, irr = flat[0:6, :], flat[8:14, :]

    result[8:14, 0:act_dev] = irr
    for k in range(1, n_blk):
        out_copy(k).wait_recv()
        left = (k % per_pack) * act_dev
        reg = reg + out_rx[k][0:6, left : left + act_dev]
    result[0:6, 0:act_dev] = reg
    total = reg + irr
    accel_now, jerk_now = total[0:3], total[3:6]
    mine = own_old[:, 0:act_dev]
    start_accel, start_jerk, step = mine[0:3], mine[3:6], mine[6:7]
    change = start_accel - accel_now
    result[16:19, 0:act_dev] = -6.0 * change - step * (4.0 * start_jerk + 2.0 * jerk_now)
    result[19:22, 0:act_dev] = 12.0 * change + 6.0 * step * (start_jerk + jerk_now)

    for k in range(1, n_blk):
        tgt_copy(k).wait_send()
        out_copy(k).wait_send()
    for k in range(1, n_grp):
        src_copy(k).wait_send()


def write_out(result, regular, irregular, correction):
    act_dev = regular.shape[1]
    regular[...] = result[0:6, 0:act_dev]
    irregular[...] = result[8:14, 0:act_dev]
    correction[...] = result[16:22, 0:act_dev]


def per_device(
    n_blk, n_grp,
    position, velocity, accel_old, jerk_old, elapsed, masses,
    active_stars, neighbour_list, neighbour_count,
):
    act_dev = active_stars.shape[0]
    res_dev = position.shape[1]
    packs = n_blk * act_dev // LANES
    shape = jax.ShapeDtypeStruct((6, act_dev), jnp.float32)
    vmem = pl.BlockSpec(memory_space=pltpu.VMEM)
    f32 = jnp.float32
    result = pl.pallas_call(
        functools.partial(kernel, n_blk, n_grp),
        out_shape=pltpu.VMEM((24, LANES), f32),
        in_specs=[pl.BlockSpec(memory_space=pltpu.HBM)] * 9,
        out_specs=vmem,
        scratch_shapes=[
            pltpu.VMEM(position.shape, f32),
            pltpu.VMEM(position.shape, f32),
            pltpu.VMEM(position.shape, f32),
            pltpu.VMEM(position.shape, f32),
            pltpu.VMEM((1, res_dev), f32),
            pltpu.VMEM((1, res_dev), f32),
            pltpu.VMEM((1, act_dev), jnp.int32),
            pltpu.VMEM(neighbour_list.shape, jnp.int32),
            pltpu.SMEM((1,), jnp.int32),
            pltpu.SemaphoreType.DMA((9,)),
            pltpu.VMEM((n_grp, 8, res_dev), f32),
            pltpu.VMEM((n_blk, 8, LANES), f32),
            pltpu.VMEM((6, packs * LANES, LANES), f32),
            pltpu.VMEM((6, packs * LANES, LANES), f32),
            pltpu.VMEM((6, act_dev, LANES), f32),
            pltpu.VMEM((n_grp * res_dev // BLOCK, LANES), f32),
            pltpu.VMEM((packs, 8, LANES), f32),
            pltpu.VMEM((n_blk, 8, LANES), f32),
            pltpu.SemaphoreType.DMA((n_grp,)),
            pltpu.SemaphoreType.DMA((n_grp,)),
            pltpu.SemaphoreType.DMA((n_blk,)),
            pltpu.SemaphoreType.DMA((n_blk,)),
            pltpu.SemaphoreType.DMA((n_blk,)),
            pltpu.SemaphoreType.DMA((n_blk,)),
        ],
        compiler_params=pltpu.CompilerParams(collective_id=0, has_side_effects=True),
        cost_estimate=pl.CostEstimate(
            flops=40 * n_blk * act_dev * n_grp * res_dev,
            bytes_accessed=32 * res_dev * n_grp,
            transcendentals=n_blk * act_dev * n_grp * res_dev,
        ),
    )(
        position, velocity, accel_old, jerk_old,
        elapsed.reshape(1, -1), masses.reshape(1, -1), active_stars.reshape(1, -1),
        neighbour_list, neighbour_count,
    )
    return pl.pallas_call(
        write_out,
        out_shape=(shape, shape, shape),
        in_specs=[vmem],
        out_specs=(vmem, vmem, vmem),
    )(pltpu.with_memory_space_constraint(result, pltpu.VMEM))


def solution(mesh):
    stars = P(None, ("blk", "grp"))
    flat = P(("blk", "grp"))
    return jax.shard_map(
        functools.partial(per_device, mesh.shape["blk"], mesh.shape["grp"]),
        mesh=mesh,
        in_specs=(stars,) * 4 + (flat,) * 3 + (P(("blk", "grp"), None), flat),
        out_specs=(stars,) * 3,
        check_vma=False,
    )
```
